32 devices in a mesh: layer: 4 (over x, core), angle: 8 (over z, y).
Axes of the slice: x: 2, y: 2, z: 4, core: 2. Of those that a mesh axis runs over, the one named last changes fastest.
Arguments:
- right_side: bfloat16 [8, 2048, 2, 96], P('layer', 'angle'), may hold values from -6 to 6
- inverse: bfloat16 [8, 2, 2048, 2048], P('layer', None, 'angle'), may hold values from -0.09375 to 0.09375
- coupling: bfloat16 [8, 4, 2, 2048, 2048], P('layer', None, None, 'angle'), may hold values from -0.046875 to 0.046875
- image_offset: int32 [8, 4], P('layer'), may hold values from 1 to 2
- image_count: int32 [8], P('layer'), may hold values from 2 to 4
- phase_exponent: int32 [8, 4], P('layer'), may hold values from -6 to 6
Outputs:
- solution: bfloat16 [8, 2048, 2, 96], P('layer', 'angle')
The draws below stay inside these ranges and needn't reach their ends.
Inputs may be any that keep to these rules, and one draw needn't show every extreme that they name: Slot k of layer l couples to layer l - image_offset[l,k]; it couples to nothing when that index is below 0. Layer l uses its first image_count[l] slots.
All inputs are finite; a program needn't handle non-finite values.
Results may differ from the reference program's by a relative error of at most 0.015.
Values may be sent and summed in bfloat16 or wider, within the bound.
No kernel may reach another device: no remote copies, remote signals or barrier semaphores. Data moves between devices by JAX's collectives and lax.ppermute only.
A program may use at most 64 MiB of HBM per device.

```python
import math
import jax
import jax.numpy as jnp
from jax import lax

M = 2048
ANGLES = 16
NRHS = 6
IMAGES = 4
LAYERS = 8
COLS = 96


def place_ends(drawn, stream_key, smallest, top_value):
    longest = drawn.shape.index(max(drawn.shape))
    spots = []
    for shift in (0, 1):
        where = [jax.random.randint(jax.random.fold_in(stream_key, axis), (), 0, length) for axis, length in enumerate(drawn.shape)]
        where[longest] = (where[longest] + shift) % drawn.shape[longest]
        spots.append(tuple(where))
    return drawn.at[spots[0]].set(smallest).at[spots[1]].set(top_value)


def shard_levels(key, extent, cuts, least, largest):
    level, own = 1.0, jax.random.fold_in(key, 6)
    for position, blocks in cuts:
        heights = jnp.exp(jax.random.uniform(jax.random.fold_in(own, position), (blocks,), jnp.float32, least / len(cuts), largest / len(cuts)))
        level = level * jnp.repeat(heights, extent[position] // blocks).reshape([-1 if axis == position else 1 for axis in range(len(extent))])
    return level


def bell_draw(stream_key, dims, width, reach, split=(), held_as=jnp.bfloat16):
    result = jax.random.normal(stream_key, dims, jnp.float32) * width
    if len(split) > 0:
        result = shard_levels(stream_key, dims, split, -0.22, 0.18) * result
    return jnp.clip(result, min=-reach, max=reach).astype(held_as)


def setup_inputs(seed: int = 0) -> dict:
    seeds = jax.random.split(jax.random.key(seed), 7)
    right_side = bell_draw(seeds[0], (LAYERS, M, 2, COLS), 1.0, 6.0, ((0, 4), (1, 8)))
    inverse = bell_draw(seeds[1], (LAYERS, 2, M, M), (2 * M) ** -0.5, 0.09375, ((0, 4), (2, 8)))
    coupling = bell_draw(seeds[2], (LAYERS, IMAGES, 2, M, M), (8 * M) ** -0.5, 0.046875, ((0, 4), (3, 8)))
    image_offset = place_ends(jax.random.randint(seeds[3], (LAYERS, IMAGES), 1, 3), jax.random.fold_in(seeds[3], 1), 1, 2).astype(jnp.int32)
    image_count = place_ends(jax.random.randint(seeds[4], (LAYERS,), 2, IMAGES + 1), jax.random.fold_in(seeds[4], 1), 2, IMAGES).astype(jnp.int32)
    phase_exponent = place_ends(jax.random.randint(seeds[5], (LAYERS, IMAGES), -6, 7), jax.random.fold_in(seeds[5], 1), -6, 6).astype(jnp.int32)
    return dict(right_side=right_side, inverse=inverse, coupling=coupling, image_offset=image_offset, image_count=image_count, phase_exponent=phase_exponent)


def complex_apply(matrix_pair, field):
    real_part = jnp.dot(matrix_pair[0], field[:, 0], preferred_element_type=jnp.float32) - jnp.dot(matrix_pair[1], field[:, 1], preferred_element_type=jnp.float32)
    imag_part = jnp.dot(matrix_pair[0], field[:, 1], preferred_element_type=jnp.float32) + jnp.dot(matrix_pair[1], field[:, 0], preferred_element_type=jnp.float32)
    return real_part, imag_part


def reference(right_side, inverse, coupling, image_offset, image_count, phase_exponent):
    column_angle = (lax.iota(jnp.int32, COLS) // NRHS).astype(jnp.float32)
    earlier = jnp.zeros((M, 2, COLS), jnp.bfloat16)
    latest = jnp.zeros((M, 2, COLS), jnp.bfloat16)
    results = []
    for layer_index in range(LAYERS):
        accumulated = right_side[layer_index].astype(jnp.float32)
        for slot_index in range(IMAGES):
            source = jnp.where(image_offset[layer_index, slot_index] == 1, latest, earlier)
            real_part, imag_part = complex_apply(coupling[layer_index, slot_index], source)
            phase_angle = (2.0 * math.pi / ANGLES) * phase_exponent[layer_index, slot_index].astype(jnp.float32) * (column_angle + 0.5)
            cosine = jnp.cos(phase_angle)
            sine = jnp.sin(phase_angle)
            image_term = jnp.stack([real_part * cosine - imag_part * sine, real_part * sine + imag_part * cosine], 1)
            accumulated = accumulated - jnp.where(image_count[layer_index] > slot_index, image_term, jnp.zeros_like(image_term))
        residual = accumulated.astype(jnp.bfloat16)
        real_part, imag_part = complex_apply(inverse[layer_index], residual)
        layer_field = jnp.stack([real_part, imag_part], 1).astype(jnp.bfloat16)
        results.append(layer_field)
        earlier = latest
        latest = layer_field
    return jnp.stack(results)
```

```python
import functools
import math

import jax
import jax.numpy as jnp
from jax import lax
from jax.experimental import pallas as pl
from jax.experimental.pallas import tpu as pltpu
from jax.sharding import PartitionSpec as P

ANGLES = 16
NRHS = 6
LIMIT = 24 * 2**20

VMEM = pl.BlockSpec(memory_space=pltpu.VMEM)
SMEM = pl.BlockSpec(memory_space=pltpu.SMEM)


def send(array, source, target, turn):
    peers = lax.axis_size("angle")
    pairs = [(source * peers + b, target * peers + (b + turn) % peers) for b in range(peers)]
    return lax.ppermute(array, ("layer", "angle"), pairs)


def gather(array, source, target):
    peers = lax.axis_size("angle")
    return [
        array if source == target and turn == 0 else send(array, source, target, turn)
        for turn in range(peers)
    ]


def assemble(state_ref, piece_refs, full_ref):
    peers = len(piece_refs)
    width = piece_refs[0].shape[1]
    me = state_ref[0]
    for turn, piece_ref in enumerate(piece_refs):
        owner = lax.rem(me - turn + peers, peers)
        full_ref[:, pl.ds(pl.multiple_of(owner * width, width), width)] = piece_ref[...]


def complex_product(full, weights):
    rows = weights.shape[1]
    cols = full.shape[0] // 2
    product = lax.dot_general(
        full,
        weights.reshape(2 * rows, weights.shape[2]),
        (((1,), (1,)), ((), ())),
        preferred_element_type=jnp.float32,
    )
    real = product[:cols, :rows] - product[cols:, rows:]
    imag = product[cols:, :rows] + product[:cols, rows:]
    return real, imag


def image_kernel(
    layer, wanted, last, pieces, state_ref, offset_ref, count_ref, base_ref, table_ref, weight_ref, *refs
):
    piece_refs, out_refs = refs[:pieces], refs[pieces:]
    out_ref = out_refs[0]
    rows = base_ref.shape[1]
    cols = base_ref.shape[0] // 2

    @pl.when(state_ref[1] == 1)
    def _():
        if pieces > 1:
            full_ref = out_refs[1]
            total_ref = out_refs[2]
            assemble(state_ref, piece_refs, full_ref)
        else:
            full_ref = piece_refs[0]
            total_ref = out_ref
        total_ref[...] = base_ref[...].astype(jnp.float32)
        for slot in range(weight_ref.shape[1]):

            @pl.when((offset_ref[layer, slot] == wanted) & (count_ref[layer] > slot))
            def _(slot=slot):
                real, imag = complex_product(full_ref[...], weight_ref[layer, slot])
                spread = (cols, rows)
                cosine = jnp.broadcast_to(table_ref[layer, slot, 0][:, :1], spread)
                sine = jnp.broadcast_to(table_ref[layer, slot, 1][:, :1], spread)
                total_ref[:cols] -= real * cosine - imag * sine
                total_ref[cols:] -= real * sine + imag * cosine

        if last:
            out_ref[...] = total_ref[...].astype(jnp.bfloat16)


def inverse_kernel(layer, pieces, state_ref, weight_ref, *refs):
    piece_refs, out_ref, full_ref = refs[:pieces], refs[pieces], refs[pieces + 1]
    cols = out_ref.shape[0] // 2

    @pl.when(state_ref[1] == 1)
    def _():
        assemble(state_ref, piece_refs, full_ref)
        real, imag = complex_product(full_ref[...], weight_ref[layer])
        out_ref[:cols] = real.astype(jnp.bfloat16)
        out_ref[cols:] = imag.astype(jnp.bfloat16)


def local(right_side, inverse, coupling, image_offset, image_count, phase_exponent):
    layers, rows, _, cols = right_side.shape
    unknowns = inverse.shape[3]
    slots = coupling.shape[1]
    sections = lax.axis_size("layer")
    position = lax.axis_index("layer")
    me = lax.axis_index("angle")
    total_layers = layers * sections
    wide = 2 * cols

    right = right_side.transpose(0, 2, 3, 1).reshape(layers, wide, rows)
    angle = (lax.iota(jnp.int32, cols) // NRHS).astype(jnp.float32)
    phase = (2.0 * math.pi / ANGLES) * phase_exponent.astype(jnp.float32)[:, :, None] * (angle + 0.5)
    table = jnp.stack([jnp.cos(phase), jnp.sin(phase)], 2)
    table = jnp.broadcast_to(table[..., None], table.shape + (128,))
    coupling = pltpu.with_memory_space_constraint(coupling, pltpu.VMEM)
    inverse = pltpu.with_memory_space_constraint(inverse, pltpu.VMEM)

    shard = jax.ShapeDtypeStruct((wide, rows), jnp.bfloat16)
    params = pltpu.CompilerParams(vmem_limit_bytes=LIMIT)
    image_cost = pl.CostEstimate(
        flops=4 * wide * rows * unknowns * 2,
        bytes_accessed=4 * 2 * rows * unknowns,
        transcendentals=0,
    )
    inverse_cost = pl.CostEstimate(
        flops=4 * wide * rows * unknowns, bytes_accessed=4 * rows * unknowns, transcendentals=0
    )

    def images(state, layer, wanted, base, pieces):
        last = len(pieces) > 1
        out_shape = [shard, jax.ShapeDtypeStruct((wide, unknowns), jnp.bfloat16)]
        scratch = [pltpu.VMEM((wide, rows), jnp.float32)]
        if not last:
            out_shape = [jax.ShapeDtypeStruct((wide, rows), jnp.float32)]
            scratch = []
        return pl.pallas_call(
            functools.partial(image_kernel, layer, wanted, last, len(pieces)),
            out_shape=out_shape,
            in_specs=[SMEM] * 3 + [VMEM] * (3 + len(pieces)),
            out_specs=[VMEM] * len(out_shape),
            scratch_shapes=scratch,
            compiler_params=params,
            cost_estimate=image_cost,
            name="images_%d" % wanted,
        )(state, image_offset, image_count, base, table, coupling, *pieces)

    def invert(state, layer, pieces):
        return pl.pallas_call(
            functools.partial(inverse_kernel, layer, len(pieces)),
            out_shape=shard,
            in_specs=[SMEM] + [VMEM] * (1 + len(pieces)),
            out_specs=VMEM,
            scratch_shapes=[pltpu.VMEM((wide, unknowns), jnp.bfloat16)],
            compiler_params=params,
            cost_estimate=inverse_cost,
            name="invert",
        )(state, inverse, *pieces)

    found = [None] * layers
    pieces = earlier = None
    for step in range(total_layers):
        section, layer = divmod(step, layers)
        state = jnp.stack([me, (position == section).astype(jnp.int32)])
        residual = base = right[layer]
        full = None
        if step >= 2:
            base = images(state, layer, 2, base, [earlier])[0]
        if step >= 1:
            residual, full = images(state, layer, 1, base, pieces)
        field = invert(state, layer, gather(residual, section, section))
        found[layer] = field if section == 0 else jnp.where(position == section, field, found[layer])
        if step + 1 < total_layers:
            following = (step + 1) // layers
            pieces = gather(field, section, following)
            earlier = full
            if full is not None and following != section:
                earlier = send(full, section, following, 0)
    return jnp.stack(found).reshape(layers, 2, cols, rows).transpose(0, 3, 1, 2)


def solution(mesh):
    placed = (
        P("layer", "angle", None, None),
        P("layer", None, "angle", None),
        P("layer", None, None, "angle", None),
        P("layer", None),
        P("layer"),
        P("layer", None),
    )
    return jax.shard_map(
        local,
        mesh=mesh,
        in_specs=placed,
        out_specs=P("layer", "angle", None, None),
        check_vma=False,
    )
```

```python
import functools
import math

import jax
import jax.numpy as jnp
from jax import lax
from jax.experimental import pallas as pl
from jax.experimental.pallas import tpu as pltpu
from jax.sharding import PartitionSpec as P

ANGLES = 16
NRHS = 6
LIMIT = 24 * 2**20

VMEM = pl.BlockSpec(memory_space=pltpu.VMEM)
SMEM = pl.BlockSpec(memory_space=pltpu.SMEM)


def shift(array, source, target):
    peers = lax.axis_size("angle")
    pairs = [(source * peers + b, target * peers + b) for b in range(peers)]
    return lax.ppermute(array, ("layer", "angle"), pairs)


def exchange(array):
    copies = jnp.broadcast_to(array[None], (lax.axis_size("angle"),) + array.shape)
    return lax.all_to_all(copies, "angle", 0, 0)


def gather(array):
    return lax.all_gather(array, "angle", axis=0)


def assemble(pieces_ref, full_ref):
    width = pieces_ref.shape[2]
    for owner in range(pieces_ref.shape[0]):
        full_ref[:, owner * width : (owner + 1) * width] = pieces_ref[owner]


def load_kernel(inverse_ref, coupling_ref, inverse_out, coupling_out, sems):
    first = pltpu.make_async_copy(inverse_ref, inverse_out, sems.at[0])
    second = pltpu.make_async_copy(coupling_ref, coupling_out, sems.at[1])
    first.start()
    second.start()
    first.wait()
    second.wait()


def complex_product(full, weights):
    rows = weights.shape[1]
    cols = full.shape[0] // 2
    product = lax.dot_general(
        full,
        weights.reshape(2 * rows, weights.shape[2]),
        (((1,), (1,)), ((), ())),
        preferred_element_type=jnp.float32,
    )
    real = product[:cols, :rows] - product[cols:, rows:]
    imag = product[cols:, :rows] + product[:cols, rows:]
    return real, imag


def image_kernel(
    layer, wanted, last, active_ref, offset_ref, count_ref, base_ref, table_ref, weight_ref, source_ref, out_ref, *refs
):
    rows = base_ref.shape[1]
    cols = base_ref.shape[0] // 2

    @pl.when(active_ref[0] == 1)
    def _():
        if last:
            full_ref, total_ref = refs
            assemble(source_ref, full_ref)
        else:
            full_ref = source_ref
            total_ref = out_ref
        total_ref[...] = base_ref[...].astype(jnp.float32)
        for slot in range(weight_ref.shape[1]):

            @pl.when((offset_ref[layer, slot] == wanted) & (count_ref[layer] > slot))
            def _(slot=slot):
                real, imag = complex_product(full_ref[...], weight_ref[layer, slot])
                spread = (cols, rows)
                cosine = jnp.broadcast_to(table_ref[layer, slot, 0][:, :1], spread)
                sine = jnp.broadcast_to(table_ref[layer, slot, 1][:, :1], spread)
                total_ref[:cols] -= real * cosine - imag * sine
                total_ref[cols:] -= real * sine + imag * cosine

        if last:
            out_ref[...] = total_ref[...].astype(jnp.bfloat16)


def inverse_kernel(layer, active_ref, weight_ref, source_ref, out_ref, full_ref):
    cols = out_ref.shape[0] // 2

    @pl.when(active_ref[0] == 1)
    def _():
        assemble(source_ref, full_ref)
        real, imag = complex_product(full_ref[...], weight_ref[layer])
        out_ref[:cols] = real.astype(jnp.bfloat16)
        out_ref[cols:] = imag.astype(jnp.bfloat16)


def local(right_side, inverse, coupling, image_offset, image_count, phase_exponent):
    layers, rows, _, cols = right_side.shape
    unknowns = inverse.shape[3]
    slots = coupling.shape[1]
    sections = lax.axis_size("layer")
    position = lax.axis_index("layer")
    total_layers = layers * sections
    wide = 2 * cols

    right = right_side.transpose(0, 2, 3, 1).reshape(layers, wide, rows)
    angle = (lax.iota(jnp.int32, cols) // NRHS).astype(jnp.float32)
    phase = (2.0 * math.pi / ANGLES) * phase_exponent.astype(jnp.float32)[:, :, None] * (angle + 0.5)
    table = jnp.stack([jnp.cos(phase), jnp.sin(phase)], 2)
    table = jnp.broadcast_to(table[..., None], table.shape + (128,))
    inverse, coupling = pl.pallas_call(
        load_kernel,
        out_shape=[pltpu.VMEM(inverse.shape, inverse.dtype), pltpu.VMEM(coupling.shape, coupling.dtype)],
        in_specs=[pl.BlockSpec(memory_space=pl.ANY)] * 2,
        out_specs=[VMEM] * 2,
        scratch_shapes=[pltpu.SemaphoreType.DMA((2,))],
        compiler_params=pltpu.CompilerParams(vmem_limit_bytes=2**20),
        name="load",
    )(pltpu.with_memory_space_constraint(inverse, pltpu.HBM), pltpu.with_memory_space_constraint(coupling, pltpu.HBM))
    coupling = pltpu.with_memory_space_constraint(coupling, pltpu.VMEM)
    inverse = pltpu.with_memory_space_constraint(inverse, pltpu.VMEM)

    shard = jax.ShapeDtypeStruct((wide, rows), jnp.bfloat16)
    params = pltpu.CompilerParams(vmem_limit_bytes=LIMIT)
    image_cost = pl.CostEstimate(
        flops=4 * wide * rows * unknowns * 2,
        bytes_accessed=4 * 2 * rows * unknowns,
        transcendentals=0,
    )
    inverse_cost = pl.CostEstimate(
        flops=4 * wide * rows * unknowns, bytes_accessed=4 * rows * unknowns, transcendentals=0
    )

    def images(active, layer, wanted, base, source):
        last = source.ndim == 3
        out_shape = [shard, jax.ShapeDtypeStruct((wide, unknowns), jnp.bfloat16)]
        scratch = [pltpu.VMEM((wide, rows), jnp.float32)]
        if not last:
            out_shape = [jax.ShapeDtypeStruct((wide, rows), jnp.float32)]
            scratch = []
        return pl.pallas_call(
            functools.partial(image_kernel, layer, wanted, last),
            out_shape=out_shape,
            in_specs=[SMEM] * 3 + [VMEM] * 4,
            out_specs=[VMEM] * len(out_shape),
            scratch_shapes=scratch,
            compiler_params=params,
            cost_estimate=image_cost,
            name="images_%d" % wanted,
        )(active, image_offset, image_count, base, table, coupling, source)

    def invert(active, layer, source):
        return pl.pallas_call(
            functools.partial(inverse_kernel, layer),
            out_shape=shard,
            in_specs=[SMEM] + [VMEM] * 2,
            out_specs=VMEM,
            scratch_shapes=[pltpu.VMEM((wide, unknowns), jnp.bfloat16)],
            compiler_params=params,
            cost_estimate=inverse_cost,
            name="invert",
        )(active, inverse, source)

    found = [None] * layers
    pieces = earlier = None
    for step in range(total_layers):
        section, layer = divmod(step, layers)
        active = (position == section).astype(jnp.int32)[None]
        residual = base = right[layer]
        full = None
        if step >= 2:
            base = images(active, layer, 2, base, earlier)[0]
        if step >= 1:
            residual, full = images(active, layer, 1, base, pieces)
        field = invert(active, layer, exchange(residual))
        found[layer] = field if section == 0 else jnp.where(position == section, field, found[layer])
        if step + 1 < total_layers:
            following = (step + 1) // layers
            if following != section:
                field = shift(field, section, following)
            pieces = gather(field)
            earlier = full
            if full is not None and following != section:
                earlier = shift(full, section, following)
    return jnp.stack(found).reshape(layers, 2, cols, rows).transpose(0, 3, 1, 2)


def solution(mesh):
    placed = (
        P("layer", "angle", None, None),
        P("layer", None, "angle", None),
        P("layer", None, None, "angle", None),
        P("layer", None),
        P("layer"),
        P("layer", None),
    )
    return jax.shard_map(
        local,
        mesh=mesh,
        in_specs=placed,
        out_specs=P("layer", "angle", None, None),
        check_vma=False,
    )
```

```python
import functools
import math

import jax
import jax.numpy as jnp
from jax import lax
from jax.experimental import pallas as pl
from jax.experimental.pallas import tpu as pltpu
from jax.sharding import PartitionSpec as P

ANGLES = 16
NRHS = 6
FRONTS = 1
LIMIT = 16 * 2**20

VMEM = pl.BlockSpec(memory_space=pltpu.VMEM)
SMEM = pl.BlockSpec(memory_space=pltpu.SMEM)
ANY = pl.BlockSpec(memory_space=pl.ANY)


def held(array):
    return pltpu.with_memory_space_constraint(array, pltpu.VMEM)


def load_kernel(source_ref, out_ref, sem):
    copy = pltpu.make_async_copy(source_ref, out_ref, sem)
    copy.start()
    copy.wait()


def load(array, name):
    return pl.pallas_call(
        load_kernel,
        out_shape=pltpu.VMEM(array.shape, array.dtype),
        in_specs=[ANY],
        out_specs=VMEM,
        scratch_shapes=[pltpu.SemaphoreType.DMA],
        compiler_params=pltpu.CompilerParams(vmem_limit_bytes=2**20),
        cost_estimate=pl.CostEstimate(flops=0, bytes_accessed=2 * array.size * 2, transcendentals=0),
        name=name,
    )(pltpu.with_memory_space_constraint(array, pltpu.HBM))


def pack_kernel(*refs):
    place = 0
    for ref in refs[:-1]:
        blocks = ref[...].reshape((-1,) + ref.shape[-2:])
        refs[-1][place : place + blocks.shape[0]] = blocks
        place += blocks.shape[0]


def pack(*parts):
    shape = parts[0].shape[-2:]
    blocks = sum(part.size for part in parts) // (shape[0] * shape[1])
    return pl.pallas_call(
        pack_kernel,
        out_shape=jax.ShapeDtypeStruct((blocks,) + shape, parts[0].dtype),
        in_specs=[VMEM] * len(parts),
        out_specs=VMEM,
        compiler_params=pltpu.CompilerParams(vmem_limit_bytes=LIMIT),
        name="pack",
    )(*parts)


def swap(array, sections, bit):
    peers = lax.axis_size("angle")
    pairs = [(s * peers + b, s * peers + (b ^ bit)) for s in sections for b in range(peers)]
    return lax.ppermute(array, ("layer", "angle"), pairs)


def shift(array, sections):
    peers = lax.axis_size("angle")
    pairs = [(s * peers + b, (s + 1) * peers + b) for s in sections for b in range(peers)]
    return lax.ppermute(array, ("layer", "angle"), pairs)


def gather(block, sections):
    peers = lax.axis_size("angle")
    far = peers // 2
    buffers = [pack(block, swap(block, sections, far))]
    turns = [(0, far)]
    bit = 1
    while bit < far:
        buffers += [swap(buffer, sections, bit) for buffer in list(buffers)]
        turns += [(a ^ bit, b ^ bit) for a, b in turns]
        bit *= 2
    return buffers, turns


def multiply(state_ref, buffer_refs, turns, weights, total):
    me = state_ref[0]
    for buffer_ref, group in zip(buffer_refs, turns):
        for place, turn in enumerate(group):
            block = buffer_ref[place]
            width = block.shape[1]
            owner = jnp.bitwise_xor(me, turn)
            part = weights[:, :, pl.ds(pl.multiple_of(owner * width, width), width)]
            product = lax.dot_general(
                block,
                part.reshape(-1, width),
                (((1,), (1,)), ((), ())),
                preferred_element_type=jnp.float32,
            )
            total = product if total is None else total + product
    return total


def complex_parts(product):
    cols, rows = product.shape[0] // 2, product.shape[1] // 2
    real = product[:cols, :rows] - product[cols:, rows:]
    imag = product[cols:, :rows] + product[:cols, rows:]
    return real, imag


def image_kernel(layer, step, wanted, turns, first, last, state_ref, offset_ref, count_ref, table_ref, weight_ref, base_ref, *refs):
    buffer_refs, out_ref = refs[: len(turns)], refs[len(turns)]
    total_ref = refs[len(turns) + 1] if last else out_ref
    cols, rows = out_ref.shape[0] // 2, out_ref.shape[1]
    front = jnp.clip(step - state_ref[1], 0, table_ref.shape[3] - 1)
    base = base_ref[layer, front] if first else base_ref[...]
    total_ref[...] = base.astype(jnp.float32)
    for slot in range(weight_ref.shape[1]):

        @pl.when((offset_ref[layer, slot] == wanted) & (count_ref[layer] > slot))
        def _(slot=slot):
            product = multiply(state_ref, buffer_refs, turns, weight_ref.at[layer, slot], None)
            real, imag = complex_parts(product)
            spread = (cols, rows)
            cosine = jnp.broadcast_to(table_ref[layer, slot, 0, front][:, :1], spread)
            sine = jnp.broadcast_to(table_ref[layer, slot, 1, front][:, :1], spread)
            total_ref[:cols] -= real * cosine - imag * sine
            total_ref[cols:] -= real * sine + imag * cosine

    if last:
        out_ref[...] = total_ref[...].astype(out_ref.dtype)


def early_inverse_kernel(layer, turns, state_ref, weight_ref, *refs):
    refs[-1][...] = multiply(state_ref, refs[:-1], turns, weight_ref.at[layer], None)


def late_inverse_kernel(layer, turns, state_ref, weight_ref, total_ref, *refs):
    product = multiply(state_ref, refs[:-1], turns, weight_ref.at[layer], total_ref[...])
    real, imag = complex_parts(product)
    cols = real.shape[0]
    refs[-1][:cols] = real.astype(jnp.bfloat16)
    refs[-1][cols:] = imag.astype(jnp.bfloat16)


def local(right_side, inverse, coupling, image_offset, image_count, phase_exponent):
    layers, rows, _, cols = right_side.shape
    slots = coupling.shape[1]
    sections = lax.axis_size("layer")
    steps = sections + FRONTS - 1
    width = cols // FRONTS
    wide = 2 * width

    inverse = held(load(inverse, "load_inverse"))
    coupling = held(load(coupling, "load_coupling"))
    state = jnp.stack([lax.axis_index("angle"), lax.axis_index("layer")])
    right = right_side.reshape(layers, rows, 2, FRONTS, width).transpose(0, 3, 2, 4, 1)
    right = right.reshape(layers, FRONTS, wide, rows)
    angle = (lax.iota(jnp.int32, cols) // NRHS).astype(jnp.float32)
    phase = (2.0 * math.pi / ANGLES) * phase_exponent.astype(jnp.float32)[:, :, None] * (angle + 0.5)
    table = jnp.stack([jnp.cos(phase), jnp.sin(phase)], 2).reshape(layers, slots, 2, FRONTS, width, 1)
    table = jnp.broadcast_to(table, table.shape[:-1] + (128,))

    params = pltpu.CompilerParams(vmem_limit_bytes=LIMIT)
    block_shape = jax.ShapeDtypeStruct((wide, rows), jnp.bfloat16)

    def cost(blocks, planes):
        return pl.CostEstimate(
            flops=4 * wide * rows * rows * blocks * planes,
            bytes_accessed=4 * rows * rows * blocks * planes,
            transcendentals=0,
        )

    def images(layer, step, wanted, base, buffers, turns, last):
        first = base.ndim == 4
        kernel = functools.partial(image_kernel, layer, step, wanted, turns, first, last)
        return pl.pallas_call(
            kernel,
            out_shape=block_shape if last else jax.ShapeDtypeStruct((wide, rows), jnp.float32),
            in_specs=[SMEM] * 3 + [VMEM] * (3 + len(buffers)),
            out_specs=VMEM,
            scratch_shapes=[pltpu.VMEM((wide, rows), jnp.float32)] if last else [],
            compiler_params=params,
            cost_estimate=cost(sum(map(len, turns)), 2),
            name="images_%d_%s" % (wanted, "late" if last else "early"),
        )(state, image_offset, image_count, table, coupling, base, *buffers)

    def early_inverse(layer, buffers, turns):
        return pl.pallas_call(
            functools.partial(early_inverse_kernel, layer, turns),
            out_shape=jax.ShapeDtypeStruct((wide, 2 * rows), jnp.float32),
            in_specs=[SMEM] + [VMEM] * (1 + len(buffers)),
            out_specs=VMEM,
            compiler_params=params,
            cost_estimate=cost(sum(map(len, turns)), 1),
            name="inverse_early",
        )(state, inverse, *buffers)

    def late_inverse(layer, total, buffers, turns):
        return pl.pallas_call(
            functools.partial(late_inverse_kernel, layer, turns),
            out_shape=block_shape,
            in_specs=[SMEM] + [VMEM] * (2 + len(buffers)),
            out_specs=VMEM,
            compiler_params=params,
            cost_estimate=cost(sum(map(len, turns)), 1),
            name="inverse_late",
        )(state, inverse, total, *buffers)

    first_right = lax.dynamic_index_in_dim
    found = {}
    earlier = latest = None
    for step in range(steps):
        active = [s for s in range(sections) if 0 <= step - s < FRONTS]
        moving = [s for s in active if s + 1 < sections]
        front = jnp.clip(step - state[1], 0, FRONTS - 1)
        for layer in range(layers):
            base = right
            if earlier is not None:
                base = images(layer, step, 2, base, earlier[0], earlier[1], False)
            if latest is not None:
                buffers, turns = latest
                base = images(layer, step, 1, base, buffers[:-1], turns[:-1], False)
                residual = images(layer, step, 1, base, buffers[-1:], turns[-1:], True)
            else:
                residual = right[layer, 0] if FRONTS == 1 else first_right(right[layer], front, 0, False)
            buffers, turns = gather(residual, active)
            total = early_inverse(layer, buffers[:-1], turns[:-1])
            field = late_inverse(layer, total, buffers[-1:], turns[-1:])
            found[step, layer] = field
            earlier = latest
            if layer + 1 < layers:
                latest = gather(field, active)
            elif step + 1 < steps:
                after = [s + 1 for s in moving]
                latest = gather(shift(field, moving), after)
                if earlier is not None:
                    buffers, turns = earlier
                    earlier = ([shift(pack(*buffers), moving)], [sum(turns, ())])

    position = lax.axis_index("layer")
    result = []
    for layer in range(layers):
        for front in range(FRONTS):
            value = found[front, layer]
            for section in range(1, sections):
                value = jnp.where(position == section, found[section + front, layer], value)
            result.append(value)
    result = jnp.stack(result).reshape(layers, FRONTS, 2, width, rows)
    return result.transpose(0, 4, 2, 1, 3).reshape(layers, rows, 2, cols)


def solution(mesh):
    placed = (
        P("layer", "angle", None, None),
        P("layer", None, "angle", None),
        P("layer", None, None, "angle", None),
        P("layer", None),
        P("layer"),
        P("layer", None),
    )
    return jax.shard_map(
        local,
        mesh=mesh,
        in_specs=placed,
        out_specs=P("layer", "angle", None, None),
        check_vma=False,
    )
```

```python
import functools
import math

import jax
import jax.numpy as jnp
from jax import lax
from jax.experimental import pallas as pl
from jax.experimental.pallas import tpu as pltpu
from jax.sharding import PartitionSpec as P

ANGLES = 16
NRHS = 6
FRONTS = 1
ENOUGH = 2**20
LIMIT = 24 * 2**20

VMEM = pl.BlockSpec(memory_space=pltpu.VMEM)
SMEM = pl.BlockSpec(memory_space=pltpu.SMEM)
ANY = pl.BlockSpec(memory_space=pl.ANY)


def far(array):
    return pltpu.with_memory_space_constraint(array, pltpu.HBM)


def shift(array, sections):
    peers = lax.axis_size("angle")
    pairs = [(s * peers + b, (s + 1) * peers + b) for s in sections for b in range(peers)]
    return lax.ppermute(array, ("layer", "angle"), pairs)


def gather(block):
    return lax.all_gather(block, "angle", axis=0)


def padded(lines, rows, peers):
    return max(lines, -(-ENOUGH // (2 * rows * peers)))


def multiply(blocks_ref, weights):
    total = None
    for owner in range(blocks_ref.shape[0]):
        block = blocks_ref[owner]
        width = block.shape[1]
        product = lax.dot_general(
            block,
            weights[:, :, owner * width : (owner + 1) * width].reshape(-1, width),
            (((1,), (1,)), ((), ())),
            preferred_element_type=jnp.float32,
        )
        total = product if total is None else total + product
    return total


def complex_parts(product):
    cols, rows = product.shape[0] // 2, product.shape[1] // 2
    real = product[:cols, :rows] - product[cols:, rows:]
    imag = product[cols:, :rows] + product[:cols, rows:]
    return real, imag


def image_kernel(
    layer, step, wanted, first, last, state_ref, offset_ref, count_ref, table_ref, base_ref, weight_ref, blocks_ref, out_ref, weights, blocks, sems, *scratch
):
    total_ref = scratch[0] if last else out_ref
    cols, rows = total_ref.shape[0] // 2, total_ref.shape[1]
    slots = weight_ref.shape[1]
    used = [(offset_ref[layer, slot] == wanted) & (count_ref[layer] > slot) for slot in range(slots)]
    fields = pltpu.make_async_copy(blocks_ref.at[:, : 2 * cols], blocks, sems.at[slots])
    fields.start()
    copies = []
    for slot in range(slots):
        copies.append(pltpu.make_async_copy(weight_ref.at[layer, slot], weights.at[slot], sems.at[slot]))
        pl.when(used[slot])(copies[slot].start)
    front = jnp.clip(step - state_ref[1], 0, table_ref.shape[3] - 1)
    base = base_ref[layer, front] if first else base_ref[...]
    total_ref[...] = base.astype(jnp.float32)
    fields.wait()
    for slot in range(slots):

        @pl.when(used[slot])
        def _(slot=slot):
            copies[slot].wait()
            real, imag = complex_parts(multiply(blocks, weights.at[slot]))
            spread = (cols, rows)
            cosine = jnp.broadcast_to(table_ref[layer, slot, 0, front][:, :1], spread)
            sine = jnp.broadcast_to(table_ref[layer, slot, 1, front][:, :1], spread)
            total_ref[:cols] -= real * cosine - imag * sine
            total_ref[cols:] -= real * sine + imag * cosine

    if last:
        out_ref[: 2 * cols] = total_ref[...].astype(out_ref.dtype)


def inverse_kernel(layer, weight_ref, blocks_ref, out_ref, weights, blocks, sems):
    wide = blocks.shape[1]
    fields = pltpu.make_async_copy(blocks_ref.at[:, :wide], blocks, sems.at[0])
    fields.start()
    copy = pltpu.make_async_copy(weight_ref.at[layer], weights, sems.at[1])
    copy.start()
    fields.wait()
    copy.wait()
    real, imag = complex_parts(multiply(blocks, weights))
    out_ref[: wide // 2] = real.astype(jnp.bfloat16)
    out_ref[wide // 2 : wide] = imag.astype(jnp.bfloat16)


def local(right_side, inverse, coupling, image_offset, image_count, phase_exponent):
    layers, rows, _, cols = right_side.shape
    slots = coupling.shape[1]
    sections = lax.axis_size("layer")
    steps = sections + FRONTS - 1
    width = cols // FRONTS
    wide = 2 * width

    state = jnp.stack([lax.axis_index("angle"), lax.axis_index("layer")])
    right = right_side.reshape(layers, rows, 2, FRONTS, width).transpose(0, 3, 2, 4, 1)
    right = right.reshape(layers, FRONTS, wide, rows)
    angle = (lax.iota(jnp.int32, cols) // NRHS).astype(jnp.float32)
    phase = (2.0 * math.pi / ANGLES) * phase_exponent.astype(jnp.float32)[:, :, None] * (angle + 0.5)
    table = jnp.stack([jnp.cos(phase), jnp.sin(phase)], 2).reshape(layers, slots, 2, FRONTS, width, 1)
    table = jnp.broadcast_to(table, table.shape[:-1] + (128,))

    params = pltpu.CompilerParams(vmem_limit_bytes=LIMIT)
    peers = lax.axis_size("angle")
    lines = padded(wide, rows, peers)
    block_shape = jax.ShapeDtypeStruct((lines, rows), jnp.bfloat16)

    def cost(planes):
        return pl.CostEstimate(
            flops=4 * wide * rows * rows * peers * planes,
            bytes_accessed=4 * rows * rows * peers * planes,
            transcendentals=0,
        )

    unknowns = rows * peers
    blocks_scratch = pltpu.VMEM((peers, wide, rows), jnp.bfloat16)

    def images(layer, step, wanted, base, blocks, last):
        return pl.pallas_call(
            functools.partial(image_kernel, layer, step, wanted, base.ndim == 4, last),
            out_shape=block_shape if last else jax.ShapeDtypeStruct((wide, rows), jnp.float32),
            in_specs=[SMEM] * 3 + [VMEM] * 2 + [ANY] * 2,
            out_specs=VMEM,
            scratch_shapes=[
                pltpu.VMEM((slots, 2, rows, unknowns), jnp.bfloat16),
                blocks_scratch,
                pltpu.SemaphoreType.DMA((slots + 1,)),
            ]
            + ([pltpu.VMEM((wide, rows), jnp.float32)] if last else []),
            compiler_params=params,
            cost_estimate=cost(2),
            name="images_%d" % wanted,
        )(state, image_offset, image_count, table, base, far(coupling), far(blocks))

    def invert(layer, blocks):
        return pl.pallas_call(
            functools.partial(inverse_kernel, layer),
            out_shape=block_shape,
            in_specs=[ANY] * 2,
            out_specs=VMEM,
            scratch_shapes=[
                pltpu.VMEM((2, rows, unknowns), jnp.bfloat16),
                blocks_scratch,
                pltpu.SemaphoreType.DMA((2,)),
            ],
            compiler_params=params,
            cost_estimate=cost(1),
            name="invert",
        )(far(inverse), far(blocks))

    found = {}
    earlier = latest = None
    for step in range(steps):
        active = [s for s in range(sections) if 0 <= step - s < FRONTS]
        moving = [s for s in active if s + 1 < sections]
        front = jnp.clip(step - state[1], 0, FRONTS - 1)
        for layer in range(layers):
            base = right
            if earlier is not None:
                base = images(layer, step, 2, base, earlier, False)
            if latest is not None:
                residual = images(layer, step, 1, base, latest, True)
            else:
                residual = lax.dynamic_index_in_dim(right[layer], front, 0, False)
                residual = jnp.pad(residual, ((0, lines - wide), (0, 0)))
            field = invert(layer, gather(residual))
            found[step, layer] = field
            earlier = latest
            if layer + 1 < layers:
                latest = gather(field)
            elif step + 1 < steps:
                latest = gather(shift(field, moving))
                if earlier is not None:
                    earlier = shift(earlier, moving)

    position = lax.axis_index("layer")
    result = []
    for layer in range(layers):
        for front in range(FRONTS):
            value = found[front, layer]
            for section in range(1, sections):
                value = jnp.where(position == section, found[section + front, layer], value)
            result.append(value[:wide])
    result = jnp.stack(result).reshape(layers, FRONTS, 2, width, rows)
    return result.transpose(0, 4, 2, 1, 3).reshape(layers, rows, 2, cols)


def solution(mesh):
    placed = (
        P("layer", "angle", None, None),
        P("layer", None, "angle", None),
        P("layer", None, None, "angle", None),
        P("layer", None),
        P("layer"),
        P("layer", None),
    )
    return jax.shard_map(
        local,
        mesh=mesh,
        in_specs=placed,
        out_specs=P("layer", "angle", None, None),
        check_vma=False,
    )
```

```python
import functools
import math

import jax
import jax.numpy as jnp
from jax import lax
from jax.experimental import pallas as pl
from jax.experimental.pallas import tpu as pltpu
from jax.sharding import PartitionSpec as P

ANGLES = 16
NRHS = 6
LIMIT = 16 * 2**20

VMEM = pl.BlockSpec(memory_space=pltpu.VMEM)
SMEM = pl.BlockSpec(memory_space=pltpu.SMEM)
ANY = pl.BlockSpec(memory_space=pl.ANY)


def held(array):
    return pltpu.with_memory_space_constraint(array, pltpu.VMEM)


def load_kernel(source_ref, out_ref, sem):
    copy = pltpu.make_async_copy(source_ref, out_ref, sem)
    copy.start()
    copy.wait()


def load(array, name):
    return pl.pallas_call(
        load_kernel,
        out_shape=pltpu.VMEM(array.shape, array.dtype),
        in_specs=[ANY],
        out_specs=VMEM,
        scratch_shapes=[pltpu.SemaphoreType.DMA],
        compiler_params=pltpu.CompilerParams(vmem_limit_bytes=2**20),
        cost_estimate=pl.CostEstimate(flops=0, bytes_accessed=2 * array.size * 2, transcendentals=0),
        name=name,
    )(pltpu.with_memory_space_constraint(array, pltpu.HBM))


def copies_kernel(source_ref, out_ref):
    for place in range(out_ref.shape[0]):
        out_ref[place] = source_ref[...]


def copies(array, count):
    return pl.pallas_call(
        copies_kernel,
        out_shape=jax.ShapeDtypeStruct((count,) + array.shape, array.dtype),
        in_specs=[VMEM],
        out_specs=VMEM,
        compiler_params=pltpu.CompilerParams(vmem_limit_bytes=LIMIT),
        name="copies",
    )(array)


def shift(array, section):
    peers = lax.axis_size("angle")
    pairs = [(section * peers + b, (section + 1) * peers + b) for b in range(peers)]
    return lax.ppermute(array, ("layer", "angle"), pairs)


def gather(pair):
    peers = lax.axis_size("angle")
    half = peers // 2
    far = [[b, b + half] for b in range(half)]
    near = [list(range(half)), list(range(half, peers))]
    both = lax.all_to_all(pair, "angle", 0, 0, axis_index_groups=far)
    return lax.all_to_all(copies(both, half), "angle", 0, 0, axis_index_groups=near)


def assemble(blocks_ref, full_ref):
    half, sides, _, width = blocks_ref.shape
    for low in range(half):
        for high in range(sides):
            first = (high * half + low) * width
            full_ref[:, first : first + width] = blocks_ref[low, high]


def complex_product(full, weights):
    cols, rows = full.shape[0] // 2, weights.shape[1]
    product = lax.dot_general(
        full,
        weights.reshape(2 * rows, weights.shape[2]),
        (((1,), (1,)), ((), ())),
        preferred_element_type=jnp.float32,
    )
    real = product[:cols, :rows] - product[cols:, rows:]
    imag = product[cols:, :rows] + product[:cols, rows:]
    return real, imag


def image_kernel(layer, kinds, offset_ref, count_ref, table_ref, weight_ref, base_ref, *refs):
    blocks_refs, out_ref, total_ref, full_refs = refs[: len(kinds)], refs[len(kinds)], refs[len(kinds) + 1], refs[len(kinds) + 2 :]
    cols, rows = total_ref.shape[0] // 2, total_ref.shape[1]
    total_ref[...] = base_ref[layer].astype(jnp.float32)
    for kind, blocks_ref, full_ref in zip(kinds, blocks_refs, full_refs):
        assemble(blocks_ref, full_ref)
        for slot in range(weight_ref.shape[1]):

            @pl.when((offset_ref[layer, slot] == kind) & (count_ref[layer] > slot))
            def _(slot=slot, full_ref=full_ref):
                real, imag = complex_product(full_ref[...], weight_ref[layer, slot])
                spread = (cols, rows)
                cosine = jnp.broadcast_to(table_ref[layer, slot, 0][:, :1], spread)
                sine = jnp.broadcast_to(table_ref[layer, slot, 1][:, :1], spread)
                total_ref[:cols] -= real * cosine - imag * sine
                total_ref[cols:] -= real * sine + imag * cosine

    for place in range(out_ref.shape[0]):
        out_ref[place] = total_ref[...].astype(out_ref.dtype)


def inverse_kernel(layer, weight_ref, blocks_ref, out_ref, full_ref):
    assemble(blocks_ref, full_ref)
    real, imag = complex_product(full_ref[...], weight_ref[layer])
    cols = real.shape[0]
    for place in range(out_ref.shape[0]):
        out_ref[place, :cols] = real.astype(jnp.bfloat16)
        out_ref[place, cols:] = imag.astype(jnp.bfloat16)


def local(right_side, inverse, coupling, image_offset, image_count, phase_exponent):
    layers, rows, _, cols = right_side.shape
    slots, unknowns = coupling.shape[1], coupling.shape[4]
    sections = lax.axis_size("layer")
    position = lax.axis_index("layer")
    wide = 2 * cols

    inverse = load(inverse, "load_inverse")
    coupling = load(coupling, "load_coupling")
    right = right_side.transpose(0, 2, 3, 1).reshape(layers, wide, rows)
    angle = (lax.iota(jnp.int32, cols) // NRHS).astype(jnp.float32)
    phase = (2.0 * math.pi / ANGLES) * phase_exponent.astype(jnp.float32)[:, :, None] * (angle + 0.5)
    table = jnp.stack([jnp.cos(phase), jnp.sin(phase)], 2)
    table = jnp.broadcast_to(table[..., None], table.shape + (128,))

    params = pltpu.CompilerParams(vmem_limit_bytes=LIMIT)
    pair_shape = jax.ShapeDtypeStruct((2, wide, rows), jnp.bfloat16)
    full_scratch = pltpu.VMEM((wide, unknowns), jnp.bfloat16)

    def cost(planes):
        return pl.CostEstimate(
            flops=4 * wide * rows * unknowns * planes,
            bytes_accessed=4 * rows * unknowns * planes,
            transcendentals=0,
        )

    def images(layer, given, coupling):
        kinds = [kind for kind in (2, 1) if given[kind] is not None]
        return pl.pallas_call(
            functools.partial(image_kernel, layer, kinds),
            out_shape=pair_shape,
            in_specs=[SMEM] * 2 + [VMEM] * (3 + len(kinds)),
            out_specs=VMEM,
            scratch_shapes=[pltpu.VMEM((wide, rows), jnp.float32)] + [full_scratch] * len(kinds),
            compiler_params=params,
            cost_estimate=cost(slots),
            name="images",
        )(image_offset, image_count, table, held(coupling), right, *[given[kind] for kind in kinds])

    def invert(layer, blocks, inverse):
        return pl.pallas_call(
            functools.partial(inverse_kernel, layer),
            out_shape=pair_shape,
            in_specs=[VMEM] * 2,
            out_specs=VMEM,
            scratch_shapes=[full_scratch],
            compiler_params=params,
            cost_estimate=cost(1),
            name="invert",
        )(held(inverse), blocks)

    found = []
    pair = earlier = None
    for section in range(sections):

        def sweep(inverse, coupling, *carried):
            pair, earlier = (carried + (None, None))[:2]
            latest = None
            fields = []
            for layer in range(layers):
                if pair is not None:
                    earlier, latest = (earlier, gather(pair)) if layer == 0 else (latest, gather(pair))
                if latest is None:
                    residual = copies(right[layer], 2)
                else:
                    residual = images(layer, {1: latest, 2: earlier}, coupling)
                pair = invert(layer, gather(residual), inverse)
                fields.append(pair)
            return (*fields, latest)

        def rest(*_):
            return tuple(jnp.zeros(x.shape, x.dtype) for x in jax.eval_shape(sweep, inverse, coupling, *carried))

        carried = () if section == 0 else (pair, earlier)
        *fields, earlier = lax.cond(position == section, sweep, rest, inverse, coupling, *carried)
        found.append(fields)
        if section + 1 < sections:
            pair = shift(fields[-1], section)
            earlier = shift(earlier, section)

    result = []
    for layer in range(layers):
        value = found[0][layer][0]
        for section in range(1, sections):
            value = jnp.where(position == section, found[section][layer][0], value)
        result.append(value)
    result = jnp.stack(result).reshape(layers, 2, cols, rows)
    return result.transpose(0, 3, 1, 2)


def solution(mesh):
    placed = (
        P("layer", "angle", None, None),
        P("layer", None, "angle", None),
        P("layer", None, None, "angle", None),
        P("layer", None),
        P("layer"),
        P("layer", None),
    )
    return jax.shard_map(
        local,
        mesh=mesh,
        in_specs=placed,
        out_specs=P("layer", "angle", None, None),
        check_vma=False,
    )
```

```python
import functools
import math

import jax
import jax.numpy as jnp
from jax import lax
from jax.experimental import pallas as pl
from jax.experimental.pallas import tpu as pltpu
from jax.sharding import PartitionSpec as P

ANGLES = 16
NRHS = 6
CHAINS = 1
PIECES = 4
LIMIT = 24 * 2**20

VMEM = pl.BlockSpec(memory_space=pltpu.VMEM)
SMEM = pl.BlockSpec(memory_space=pltpu.SMEM)
ANY = pl.BlockSpec(memory_space=pl.ANY)


def copies_kernel(source_ref, out_ref):
    for place in range(out_ref.shape[0]):
        out_ref[place] = source_ref[...]


def copies(array, count):
    return pl.pallas_call(
        copies_kernel,
        out_shape=jax.ShapeDtypeStruct((count,) + array.shape, array.dtype),
        in_specs=[VMEM],
        out_specs=VMEM,
        compiler_params=pltpu.CompilerParams(vmem_limit_bytes=LIMIT),
        name="copies",
    )(array)


def shift(array, section):
    peers = lax.axis_size("angle")
    pairs = [(section * peers + b, (section + 1) * peers + b) for b in range(peers)]
    return lax.ppermute(array, ("layer", "angle"), pairs)


def gather(copied):
    return lax.all_to_all(copied, "angle", 0, 0)


def assemble(blocks_ref, full_ref, first_line):
    peers, lines, width = blocks_ref.shape
    for owner in range(peers):
        full_ref[first_line : first_line + lines, owner * width : (owner + 1) * width] = blocks_ref[owner]


def multiply(full, weights):
    return lax.dot_general(
        full,
        weights.reshape(-1, weights.shape[2]),
        (((1,), (1,)), ((), ())),
        preferred_element_type=jnp.float32,
    )


def complex_parts(product):
    cols, rows = product.shape[0] // 2, product.shape[1] // 2
    real = product[:cols, :rows] - product[cols:, rows:]
    imag = product[cols:, :rows] + product[:cols, rows:]
    return real, imag


def image_kernel(layer, kind, first, chains, kind_ref, table_ref, weight_ref, *refs):
    count = len(chains)
    base_refs, blocks_refs, out_refs = refs[:count], refs[count : 2 * count], refs[2 * count : 3 * count]
    total_ref, full_ref, weights, sems = refs[3 * count :]
    wide, rows = total_ref.shape[1:]
    cols = wide // 2
    slots = weight_ref.shape[1]
    used = [kind_ref[layer, slot] == kind for slot in range(slots)]
    copied = []
    for slot in range(slots):
        copied.append(pltpu.make_async_copy(weight_ref.at[layer, slot], weights.at[slot], sems.at[slot]))
        pl.when(used[slot])(copied[slot].start)
    for place, chain in enumerate(chains):
        base = base_refs[place][layer, chain] if first else base_refs[place][...]
        total_ref[place] = base.astype(jnp.float32)
        assemble(blocks_refs[place], full_ref, place * wide)
    for slot in range(slots):

        @pl.when(used[slot])
        def _(slot=slot):
            copied[slot].wait()
            product = multiply(full_ref[...], weights[slot])
            for place, chain in enumerate(chains):
                real, imag = complex_parts(product[place * wide : (place + 1) * wide])
                spread = (cols, rows)
                cosine = jnp.broadcast_to(table_ref[layer, slot, 0, chain][:, :1], spread)
                sine = jnp.broadcast_to(table_ref[layer, slot, 1, chain][:, :1], spread)
                total_ref[place, :cols] -= real * cosine - imag * sine
                total_ref[place, cols:] -= real * sine + imag * cosine

    for place, out_ref in enumerate(out_refs):
        if out_ref.ndim == 2:
            out_ref[...] = total_ref[place]
        else:
            for copy in range(out_ref.shape[0]):
                out_ref[copy] = total_ref[place].astype(jnp.bfloat16)


def inverse_kernel(layer, weight_ref, blocks_ref, out_ref, full_ref, weights, sems):
    width = weights.shape[2] // sems.shape[0]
    pieces = [pl.ds(piece * width, width) for piece in range(sems.shape[0])]
    copied = [
        pltpu.make_async_copy(weight_ref.at[layer, :, :, piece], weights.at[:, :, piece], sems.at[place])
        for place, piece in enumerate(pieces)
    ]
    for copy in copied:
        copy.start()
    assemble(blocks_ref, full_ref, 0)
    total = None
    for copy, piece in zip(copied, pieces):
        copy.wait()
        product = multiply(full_ref[:, piece], weights[:, :, piece])
        total = product if total is None else total + product
    real, imag = complex_parts(total)
    cols = real.shape[0]
    for place in range(out_ref.shape[0]):
        out_ref[place, :cols] = real.astype(jnp.bfloat16)
        out_ref[place, cols:] = imag.astype(jnp.bfloat16)


def local(right_side, inverse, coupling, image_offset, image_count, phase_exponent):
    layers, rows, _, cols = right_side.shape
    slots, unknowns = coupling.shape[1], coupling.shape[4]
    sections, peers = lax.axis_size("layer"), lax.axis_size("angle")
    position = lax.axis_index("layer")
    width = cols // CHAINS
    wide = 2 * width
    every = list(range(CHAINS))

    right = right_side.reshape(layers, rows, 2, CHAINS, width).transpose(0, 3, 2, 4, 1)
    right = right.reshape(layers, CHAINS, wide, rows)
    kinds = jnp.where(lax.iota(jnp.int32, slots) < image_count[:, None], image_offset, 0)
    angle = (lax.iota(jnp.int32, cols) // NRHS).astype(jnp.float32)
    phase = (2.0 * math.pi / ANGLES) * phase_exponent.astype(jnp.float32)[:, :, None] * (angle + 0.5)
    table = jnp.stack([jnp.cos(phase), jnp.sin(phase)], 2).reshape(layers, slots, 2, CHAINS, width, 1)
    table = jnp.broadcast_to(table, table.shape[:-1] + (128,))
    coupling = pltpu.with_memory_space_constraint(coupling, pltpu.HBM)
    inverse = pltpu.with_memory_space_constraint(inverse, pltpu.HBM)

    params = pltpu.CompilerParams(vmem_limit_bytes=LIMIT)

    def copied_shape(count):
        return jax.ShapeDtypeStruct((count, wide, rows), jnp.bfloat16)

    def cost(planes, chains):
        return pl.CostEstimate(
            flops=4 * wide * chains * rows * unknowns * planes,
            bytes_accessed=4 * rows * unknowns * planes,
            transcendentals=0,
        )

    def images(layer, kind, chains, base, blocks):
        count = len(chains)
        first = base[0].ndim == 4
        part = jax.ShapeDtypeStruct((wide, rows), jnp.float32)
        return pl.pallas_call(
            functools.partial(image_kernel, layer, kind, first, chains),
            out_shape=[part if kind == 2 else copied_shape(peers)] * count,
            in_specs=[SMEM, VMEM, ANY] + [VMEM] * (2 * count),
            out_specs=[VMEM] * count,
            scratch_shapes=[
                pltpu.VMEM((count, wide, rows), jnp.float32),
                pltpu.VMEM((count * wide, unknowns), jnp.bfloat16),
                pltpu.VMEM((slots, 2, rows, unknowns), jnp.bfloat16),
                pltpu.SemaphoreType.DMA((slots,)),
            ],
            compiler_params=params,
            cost_estimate=cost(slots // 2, count),
            name="images_%d" % kind,
        )(kinds, table, pltpu.with_memory_space_constraint(coupling, pltpu.HBM), *base, *blocks)

    def invert(layer, blocks, count):
        return pl.pallas_call(
            functools.partial(inverse_kernel, layer),
            out_shape=copied_shape(count),
            in_specs=[ANY, VMEM],
            out_specs=VMEM,
            scratch_shapes=[
                pltpu.VMEM((wide, unknowns), jnp.bfloat16),
                pltpu.VMEM((2, rows, unknowns), jnp.bfloat16),
                pltpu.SemaphoreType.DMA((PIECES,)),
            ],
            compiler_params=params,
            cost_estimate=cost(1, 1),
            name="invert",
        )(pltpu.with_memory_space_constraint(inverse, pltpu.HBM), blocks)

    found = []
    carried = ()
    for section in range(sections):

        def sweep(*carried):
            fields, earlier = carried[:CHAINS], carried[CHAINS:]
            latest = copied = ()
            if section > 0:
                copied = [copies(field, peers) for field in fields]
            out = []
            for layer in range(layers):
                base = [right] * CHAINS
                if copied:
                    earlier, latest = (earlier if layer == 0 else latest), [gather(x) for x in copied]
                    if earlier:
                        base = images(layer, 2, every, base, earlier)
                    residual = [images(layer, 1, [c], [base[c]], [latest[c]])[0] for c in every]
                else:
                    residual = [copies(right[layer, c], peers) for c in every]
                count = peers if layer + 1 < layers else 1
                copied = [invert(layer, gather(residual[c]), count) for c in every]
                out += [x[0] for x in copied]
            return (*out, *latest)

        def rest(*carried):
            return tuple(jnp.zeros(x.shape, x.dtype) for x in jax.eval_shape(sweep, *carried))

        swept = lax.cond(position == section, sweep, rest, *carried)
        fields, latest = swept[: layers * CHAINS], swept[layers * CHAINS :]
        found.append(fields)
        if section + 1 < sections:
            carried = [shift(x, section) for x in (*fields[-CHAINS:], *latest)]

    result = []
    for place in range(layers * CHAINS):
        value = found[0][place]
        for section in range(1, sections):
            value = jnp.where(position == section, found[section][place], value)
        result.append(value)
    result = jnp.stack(result).reshape(layers, CHAINS, 2, width, rows)
    return result.transpose(0, 4, 2, 1, 3).reshape(layers, rows, 2, cols)


def solution(mesh):
    placed = (
        P("layer", "angle", None, None),
        P("layer", None, "angle", None),
        P("layer", None, None, "angle", None),
        P("layer", None),
        P("layer"),
        P("layer", None),
    )
    return jax.shard_map(
        local,
        mesh=mesh,
        in_specs=placed,
        out_specs=P("layer", "angle", None, None),
        check_vma=False,
    )
```

```python
import functools
import math

import jax
import jax.numpy as jnp
from jax import lax
from jax.experimental import pallas as pl
from jax.experimental.pallas import tpu as pltpu
from jax.sharding import PartitionSpec as P

ANGLES = 16
NRHS = 6
CORES = 2
PIECES = 4
LIMIT = 24 * 2**20

VMEM = pl.BlockSpec(memory_space=pltpu.VMEM)
SMEM = pl.BlockSpec(memory_space=pltpu.SMEM)
ANY = pl.BlockSpec(memory_space=pl.ANY)


def copies_kernel(source_ref, out_ref):
    for place in range(out_ref.shape[0]):
        out_ref[place] = source_ref[...]


def copies(array, count):
    return pl.pallas_call(
        copies_kernel,
        out_shape=jax.ShapeDtypeStruct((count,) + array.shape, array.dtype),
        in_specs=[VMEM],
        out_specs=VMEM,
        compiler_params=pltpu.CompilerParams(vmem_limit_bytes=LIMIT),
        name="copies",
    )(array)


def swap(array):
    pairs = [(i, i ^ 1) for i in range(lax.axis_size("layer"))]
    return lax.ppermute(array, "layer", pairs)


def shift(array, chip):
    peers = lax.axis_size("angle")
    first, last = chip * CORES * peers, (chip + 1) * CORES * peers
    return lax.ppermute(array, ("layer", "angle"), [(i, i + CORES * peers) for i in range(first, last)])


def gather(copied):
    return lax.all_to_all(copied, "angle", 0, 0)


def assemble(blocks_ref, full_ref, first_line):
    peers, lines, width = blocks_ref.shape
    for owner in range(peers):
        full_ref[first_line : first_line + lines, owner * width : (owner + 1) * width] = blocks_ref[owner]


def multiply(full, weights):
    return lax.dot_general(
        full,
        weights.reshape(-1, weights.shape[2]),
        (((1,), (1,)), ((), ())),
        preferred_element_type=jnp.float32,
    )


def complex_parts(product):
    cols, rows = product.shape[0] // 2, product.shape[1] // 2
    real = product[:cols, :rows] - product[cols:, rows:]
    imag = product[cols:, :rows] + product[:cols, rows:]
    return real, imag


def weight_copy(own, own_ref, other_ref, index, target, sem):
    mine = pltpu.make_async_copy(own_ref.at[index], target, sem)
    given = pltpu.make_async_copy(other_ref.at[index], target, sem)

    def start(wanted):
        pl.when(wanted & own)(mine.start)
        pl.when(wanted & jnp.logical_not(own))(given.start)

    return start, mine.wait


def image_kernel(layer, kind, first, plan_ref, table_ref, own_ref, other_ref, base_ref, blocks_ref, out_ref, total_ref, full_ref, weights, sems):
    wide, rows = total_ref.shape
    cols = wide // 2
    layers, slots = own_ref.shape[:2]
    own = plan_ref[plan_ref.shape[0] - 1, 0] == layer // layers
    used = [plan_ref[layer, slot] == kind for slot in range(slots)]
    waits = []
    for slot in range(slots):
        index = (layer % layers, slot)
        start, wait = weight_copy(own, own_ref, other_ref, index, weights.at[slot], sems.at[slot])
        start(used[slot])
        waits.append(wait)
    base = base_ref[layer] if first else base_ref[...]
    total_ref[...] = base.astype(jnp.float32)
    assemble(blocks_ref, full_ref, 0)
    for slot in range(slots):

        @pl.when(used[slot])
        def _(slot=slot):
            waits[slot]()
            real, imag = complex_parts(multiply(full_ref[...], weights[slot]))
            cosine = jnp.broadcast_to(table_ref[layer, slot, 0][:, :1], (cols, rows))
            sine = jnp.broadcast_to(table_ref[layer, slot, 1][:, :1], (cols, rows))
            total_ref[:cols] -= real * cosine - imag * sine
            total_ref[cols:] -= real * sine + imag * cosine

    if out_ref.ndim == 2:
        out_ref[...] = total_ref[...]
    else:
        for copy in range(out_ref.shape[0]):
            out_ref[copy] = total_ref[...].astype(jnp.bfloat16)


def inverse_kernel(layer, plan_ref, own_ref, other_ref, blocks_ref, out_ref, full_ref, weights, sems):
    layers = own_ref.shape[0]
    own = plan_ref[plan_ref.shape[0] - 1, 0] == layer // layers
    width = weights.shape[2] // sems.shape[0]
    pieces = [pl.ds(piece * width, width) for piece in range(sems.shape[0])]
    waits = []
    for place, piece in enumerate(pieces):
        index = (layer % layers, slice(None), slice(None), piece)
        start, wait = weight_copy(own, own_ref, other_ref, index, weights.at[:, :, piece], sems.at[place])
        start(True)
        waits.append(wait)
    assemble(blocks_ref, full_ref, 0)
    total = None
    for wait, piece in zip(waits, pieces):
        wait()
        product = multiply(full_ref[:, piece], weights[:, :, piece])
        total = product if total is None else total + product
    real, imag = complex_parts(total)
    cols = real.shape[0]
    for place in range(out_ref.shape[0]):
        out_ref[place, :cols] = real.astype(jnp.bfloat16)
        out_ref[place, cols:] = imag.astype(jnp.bfloat16)


def far(array):
    return pltpu.with_memory_space_constraint(array, pltpu.HBM)


def local(right_side, inverse, coupling, image_offset, image_count, phase_exponent):
    layers, rows, _, cols = right_side.shape
    slots, unknowns = coupling.shape[1], coupling.shape[4]
    peers = lax.axis_size("angle")
    chips = lax.axis_size("layer") // CORES
    chip, core = jnp.divmod(lax.axis_index("layer"), CORES)
    deep = CORES * layers
    width = cols // CORES
    wide = 2 * width

    def ordered(mine, given):
        return jnp.where(core == 0, jnp.concatenate([mine, given]), jnp.concatenate([given, mine]))

    right = right_side.reshape(layers, rows, 2, CORES, width).transpose(3, 0, 2, 4, 1)
    right = right.reshape(CORES, layers, wide, rows)
    right = ordered(
        jnp.where(core == 0, right[0], right[1]), swap(jnp.where(core == 0, right[1], right[0]))
    )
    kinds = jnp.where(lax.iota(jnp.int32, slots) < image_count[:, None], image_offset, 0)
    both = jnp.stack([kinds, phase_exponent], 1)
    both = ordered(both, swap(both))
    right, both, late_inverse, late_coupling = lax.optimization_barrier((right, both, inverse, coupling))
    other_inverse, other_coupling = swap(late_inverse), swap(late_coupling)
    plan = jnp.concatenate([both[:, 0], jnp.full((1, slots), core, jnp.int32)])
    angle = ((core * width + lax.iota(jnp.int32, width)) // NRHS).astype(jnp.float32)
    phase = (2.0 * math.pi / ANGLES) * both[:, 1].astype(jnp.float32)[:, :, None] * (angle + 0.5)
    table = jnp.stack([jnp.cos(phase), jnp.sin(phase)], 2)
    table = jnp.broadcast_to(table[..., None], table.shape + (128,))

    params = pltpu.CompilerParams(vmem_limit_bytes=LIMIT)

    def copied_shape(count):
        return jax.ShapeDtypeStruct((count, wide, rows), jnp.bfloat16)

    def cost(planes):
        return pl.CostEstimate(
            flops=4 * wide * rows * unknowns * planes,
            bytes_accessed=4 * rows * unknowns * planes,
            transcendentals=0,
        )

    def images(layer, kind, base, blocks):
        part = jax.ShapeDtypeStruct((wide, rows), jnp.float32)
        return pl.pallas_call(
            functools.partial(image_kernel, layer, kind, base.ndim == 3),
            out_shape=part if kind == 2 else copied_shape(peers),
            in_specs=[SMEM, VMEM, ANY, ANY] + [VMEM] * 2,
            out_specs=VMEM,
            scratch_shapes=[
                pltpu.VMEM((wide, rows), jnp.float32),
                pltpu.VMEM((wide, unknowns), jnp.bfloat16),
                pltpu.VMEM((slots, 2, rows, unknowns), jnp.bfloat16),
                pltpu.SemaphoreType.DMA((slots,)),
            ],
            compiler_params=params,
            cost_estimate=cost(slots // 2),
            name="images_%d" % kind,
        )(plan, table, far(coupling), far(other_coupling), base, blocks)

    def invert(layer, blocks):
        return pl.pallas_call(
            functools.partial(inverse_kernel, layer),
            out_shape=copied_shape(peers if layer + 1 < deep else 1),
            in_specs=[SMEM, ANY, ANY, VMEM],
            out_specs=VMEM,
            scratch_shapes=[
                pltpu.VMEM((wide, unknowns), jnp.bfloat16),
                pltpu.VMEM((2, rows, unknowns), jnp.bfloat16),
                pltpu.SemaphoreType.DMA((PIECES,)),
            ],
            compiler_params=params,
            cost_estimate=cost(1),
            name="invert",
        )(plan, far(inverse), far(other_inverse), blocks)

    def sweep(first, latest, earlier):
        fields = []
        for layer in range(first, deep):
            base = right if earlier is None else images(layer, 2, right, earlier)
            copied = invert(layer, gather(images(layer, 1, base, latest)))
            fields.append(copied[0])
            if layer + 1 < deep:
                earlier, latest = latest, gather(copied)
        return (*fields, latest)

    def on_chip(number, function, *operands):
        def rest(*operands):
            shapes = jax.eval_shape(function, *operands)
            return jax.tree.map(lambda x: jnp.zeros(x.shape, x.dtype), shapes)

        return lax.cond(chip == number, function, rest, *operands)

    found = []
    field = earlier = None
    for number in range(chips):
        if number == 0:
            blocks = on_chip(0, lambda base: gather(copies(base, peers)), right[0])

            def begin(blocks):
                copied = invert(0, blocks)
                return copied[0], gather(copied)

            field, latest = on_chip(0, begin, blocks)
            *fields, latest = on_chip(0, lambda latest: sweep(1, latest, None), latest)
            fields = [field, *fields]
        else:

            def run(field, earlier):
                return sweep(0, gather(copies(field, peers)), earlier)

            *fields, latest = on_chip(number, run, field, earlier)
        found.append(fields)
        if number + 1 < chips:
            field, earlier = shift(fields[-1], number), shift(latest, number)

    chosen = []
    for layer in range(deep):
        value = found[0][layer]
        for number in range(1, chips):
            value = jnp.where(chip == number, found[number][layer], value)
        chosen.append(value)
    low, high = jnp.stack(chosen[:layers]), jnp.stack(chosen[layers:])
    mine = jnp.where(core == 0, low, high)
    given = swap(jnp.where(core == 0, high, low))
    result = jnp.where(core == 0, jnp.stack([mine, given]), jnp.stack([given, mine]))
    result = result.reshape(CORES, layers, 2, width, rows).transpose(1, 4, 2, 0, 3)
    return result.reshape(layers, rows, 2, cols)


def solution(mesh):
    placed = (
        P("layer", "angle", None, None),
        P("layer", None, "angle", None),
        P("layer", None, None, "angle", None),
        P("layer", None),
        P("layer"),
        P("layer", None),
    )
    return jax.shard_map(
        local,
        mesh=mesh,
        in_specs=placed,
        out_specs=P("layer", "angle", None, None),
        check_vma=False,
    )
```

```python
import functools
import math

import jax
import jax.numpy as jnp
from jax import lax
from jax.experimental import pallas as pl
from jax.experimental.pallas import tpu as pltpu
from jax.sharding import PartitionSpec as P

ANGLES = 16
NRHS = 6
CORES = 2
LIMIT = 24 * 2**20
PIECES = 4

VMEM = pl.BlockSpec(memory_space=pltpu.VMEM)
ANY = pl.BlockSpec(memory_space=pl.ANY)


def copies_kernel(source_ref, out_ref):
    for place in range(out_ref.shape[0]):
        out_ref[place] = source_ref[...]


def copies(array, count):
    return pl.pallas_call(
        copies_kernel,
        out_shape=jax.ShapeDtypeStruct((count,) + array.shape, array.dtype),
        in_specs=[VMEM],
        out_specs=VMEM,
        compiler_params=pltpu.CompilerParams(vmem_limit_bytes=LIMIT),
        name="copies",
    )(array)


def swap(array):
    pairs = [(i, i ^ 1) for i in range(lax.axis_size("layer"))]
    return lax.ppermute(array, "layer", pairs)


def shift(array, chip):
    peers = lax.axis_size("angle")
    first, last = chip * CORES * peers, (chip + 1) * CORES * peers
    return lax.ppermute(array, ("layer", "angle"), [(i, i + CORES * peers) for i in range(first, last)])


def gather(copied):
    return lax.all_to_all(copied, "angle", 0, 0)


def assemble(blocks_ref, full_ref, first_line):
    peers, lines, width = blocks_ref.shape
    for owner in range(peers):
        full_ref[first_line : first_line + lines, owner * width : (owner + 1) * width] = blocks_ref[owner]


def multiply(full, weights):
    return lax.dot_general(
        full,
        weights.reshape(-1, weights.shape[2]),
        (((1,), (1,)), ((), ())),
        preferred_element_type=jnp.float32,
    )


def complex_parts(product):
    cols, rows = product.shape[0] // 2, product.shape[1] // 2
    real = product[:cols, :rows] - product[cols:, rows:]
    imag = product[cols:, :rows] + product[:cols, rows:]
    return real, imag


def image_kernel(layer, local_layer, kind, first, plan_ref, table_ref, weight_ref, base_ref, blocks_ref, out_ref, total_ref, full_ref, weights, sems):
    wide, rows = total_ref.shape
    cols = wide // 2
    slots = weight_ref.shape[1]
    used = [jnp.max(plan_ref[layer, slot]) == kind for slot in range(slots)]
    copied = []
    for slot in range(slots):
        copied.append(pltpu.make_async_copy(weight_ref.at[local_layer, slot], weights.at[slot], sems.at[slot]))
        pl.when(used[slot])(copied[slot].start)
    base = base_ref[layer] if first else base_ref[...]
    total_ref[...] = base.astype(jnp.float32)
    assemble(blocks_ref, full_ref, 0)
    for slot in range(slots):

        @pl.when(used[slot])
        def _(slot=slot):
            copied[slot].wait()
            real, imag = complex_parts(multiply(full_ref[...], weights[slot]))
            cosine = jnp.broadcast_to(table_ref[layer, slot, 0][:, :1], (cols, rows))
            sine = jnp.broadcast_to(table_ref[layer, slot, 1][:, :1], (cols, rows))
            total_ref[:cols] -= real * cosine - imag * sine
            total_ref[cols:] -= real * sine + imag * cosine

    if out_ref.ndim == 2:
        out_ref[...] = total_ref[...]
    else:
        total = total_ref[...].astype(jnp.bfloat16)
        for place in range(out_ref.shape[0]):
            out_ref[place] = total


def inverse_kernel(local_layer, weight_ref, blocks_ref, field_ref, *refs):
    copied_refs, full_ref = refs[:-1], refs[-1]
    assemble(blocks_ref, full_ref, 0)
    real, imag = complex_parts(multiply(full_ref[...], weight_ref[local_layer]))
    field = jnp.concatenate([real, imag]).astype(jnp.bfloat16)
    field_ref[...] = field
    for copied_ref in copied_refs:
        for place in range(copied_ref.shape[0]):
            copied_ref[place] = field


def nothing(shapes):
    return list(
        pl.pallas_call(
            lambda *refs: None, out_shape=shapes, out_specs=[ANY] * len(shapes), name="nothing"
        )()
    )


def held(array):
    return pltpu.with_memory_space_constraint(array, pltpu.VMEM)


def far(array):
    return pltpu.with_memory_space_constraint(array, pltpu.HBM)


def local(right_side, inverse, coupling, image_offset, image_count, phase_exponent):
    layers, rows, _, cols = right_side.shape
    slots, unknowns = coupling.shape[1], coupling.shape[4]
    peers = lax.axis_size("angle")
    chips = lax.axis_size("layer") // CORES
    chip, core = jnp.divmod(lax.axis_index("layer"), CORES)
    deep = CORES * layers
    width = cols // CORES
    wide = 2 * width

    def ordered(mine, given):
        return jnp.where(core == 0, jnp.concatenate([mine, given]), jnp.concatenate([given, mine]))

    right = right_side.reshape(layers, rows, 2, CORES, width).transpose(3, 0, 2, 4, 1)
    split = right.reshape(CORES, layers, wide, rows)
    right = ordered(
        jnp.where(core == 0, split[0], split[1]), swap(jnp.where(core == 0, split[1], split[0]))
    )
    kinds = jnp.where(lax.iota(jnp.int32, slots) < image_count[:, None], image_offset, 0)
    both = jnp.stack([kinds, phase_exponent], 1)
    both = ordered(both, swap(both))
    right, both, late_inverse = lax.optimization_barrier((right, both, inverse))
    other_inverse = swap(late_inverse)
    plan = jnp.broadcast_to(both[:, 0].astype(jnp.float32)[..., None, None], (deep, slots, 8, 128))
    angle = ((core * width + lax.iota(jnp.int32, width)) // NRHS).astype(jnp.float32)
    phase = (2.0 * math.pi / ANGLES) * both[:, 1].astype(jnp.float32)[:, :, None] * (angle + 0.5)
    table = jnp.stack([jnp.cos(phase), jnp.sin(phase)], 2)
    table = jnp.broadcast_to(table[..., None], table.shape + (128,))

    params = pltpu.CompilerParams(vmem_limit_bytes=LIMIT)
    field_shape = jax.ShapeDtypeStruct((wide, rows), jnp.bfloat16)
    copied_shape = jax.ShapeDtypeStruct((peers, wide, rows), jnp.bfloat16)
    full_scratch = pltpu.VMEM((wide, unknowns), jnp.bfloat16)

    def cost(planes):
        return pl.CostEstimate(
            flops=4 * wide * rows * unknowns * planes,
            bytes_accessed=4 * rows * unknowns * planes,
            transcendentals=0,
        )

    def images(layer, side, kind, base, blocks):
        weights = coupling if layer // layers == side else other_coupling
        first = base.ndim == 3
        return pl.pallas_call(
            functools.partial(image_kernel, layer, layer % layers, kind, first),
            out_shape=copied_shape if kind == 1 else jax.ShapeDtypeStruct((wide, rows), jnp.float32),
            in_specs=[VMEM] * 2 + [ANY] + [VMEM] * 2,
            out_specs=VMEM,
            scratch_shapes=[
                pltpu.VMEM((wide, rows), jnp.float32),
                full_scratch,
                pltpu.VMEM((slots, 2, rows, unknowns), jnp.bfloat16),
                pltpu.SemaphoreType.DMA((slots,)),
            ],
            compiler_params=params,
            cost_estimate=cost(slots // 2),
            name="images_%d" % kind,
        )(plan, table, far(weights), base, blocks)

    def invert(layer, side, blocks):
        weights = inverse if layer // layers == side else other_inverse
        return pl.pallas_call(
            functools.partial(inverse_kernel, layer % layers),
            out_shape=[field_shape] + [copied_shape] * (layer + 1 < deep),
            in_specs=[VMEM] * 2,
            out_specs=[VMEM] * (1 + (layer + 1 < deep)),
            scratch_shapes=[full_scratch],
            compiler_params=params,
            cost_estimate=cost(1),
            name="invert",
        )(held(weights), blocks)

    def run(side, start, stop, blocks, latest, earlier):
        fields = []
        for layer in range(start, stop):
            if blocks is None:
                base = right if earlier is None else images(layer, side, 2, right, earlier)
                blocks = gather(images(layer, side, 1, base, latest))
            field, *copied = invert(layer, side, blocks)
            fields.append(field)
            blocks = None
            if copied:
                earlier, latest = latest, gather(copied[0])
        return fields, latest, earlier

    def on_chip(number, shapes, functions, *operands):
        which = jnp.where(chip == number, core + 1, 0)
        return lax.switch(which, [lambda *_: nothing(shapes), *functions], *operands)

    found = []
    field = earlier = None
    for number in range(chips):
        if number == 0:


            def first(start):
                return [gather(copies(start, peers))]

            (blocks,) = on_chip(0, [copied_shape], [first, first], right[0])
            blocks, late_coupling = lax.optimization_barrier((blocks, coupling))
            other_coupling = swap(late_coupling)

            def low_own(blocks):
                fields, latest, earlier = run(0, 0, layers, blocks, None, None)
                return [*fields, latest, latest if earlier is None else earlier]

            def high_first(blocks):
                fields, latest, _ = run(1, 0, 1, blocks, None, None)
                return [*fields, *(fields * (layers - 1)), latest, latest]

            shapes = [field_shape] * layers + [copied_shape] * 2
            *begun, latest, earlier = on_chip(0, shapes, [low_own, high_first], blocks)

            def low_rest(latest, earlier, *begun):
                fields, latest, _ = run(0, layers, deep, None, latest, earlier if layers > 1 else None)
                return [*begun, *fields, latest]

            def high_rest(latest, earlier, *begun):
                fields, latest, _ = run(1, 1, deep, None, latest, None)
                return [begun[0], *fields, latest]

            functions, operands = [low_rest, high_rest], (latest, earlier, *begun)
        else:

            def whole(side, field, earlier):
                fields, latest, _ = run(side, 0, deep, None, gather(copies(field, peers)), earlier)
                return [*fields, latest]

            functions = [functools.partial(whole, side) for side in range(CORES)]
            operands = (field, earlier)
        shapes = [field_shape] * deep + [copied_shape]
        *fields, latest = on_chip(number, shapes, functions, *operands)
        found.append(fields)
        if number + 1 < chips:
            field, earlier = shift(fields[-1], number), shift(latest, number)

    chosen = []
    for layer in range(deep):
        value = found[0][layer]
        for number in range(1, chips):
            value = jnp.where(chip == number, found[number][layer], value)
        chosen.append(value)
    low, high = jnp.stack(chosen[:layers]), jnp.stack(chosen[layers:])
    mine = jnp.where(core == 0, low, high)
    given = swap(jnp.where(core == 0, high, low))
    result = jnp.where(core == 0, jnp.stack([mine, given]), jnp.stack([given, mine]))
    result = result.reshape(CORES, layers, 2, width, rows).transpose(1, 4, 2, 0, 3)
    return result.reshape(layers, rows, 2, cols)


def solution(mesh):
    placed = (
        P("layer", "angle", None, None),
        P("layer", None, "angle", None),
        P("layer", None, None, "angle", None),
        P("layer", None),
        P("layer"),
        P("layer", None),
    )
    return jax.shard_map(
        local,
        mesh=mesh,
        in_specs=placed,
        out_specs=P("layer", "angle", None, None),
        check_vma=False,
    )
```

```python
import functools
import math

import jax
import jax.numpy as jnp
from jax import lax
from jax.experimental import pallas as pl
from jax.experimental.pallas import tpu as pltpu
from jax.sharding import PartitionSpec as P

ANGLES = 16
NRHS = 6
CORES = 2
LIMIT = 24 * 2**20

VMEM = pl.BlockSpec(memory_space=pltpu.VMEM)
ANY = pl.BlockSpec(memory_space=pl.ANY)


def copies_kernel(source_ref, out_ref):
    for place in range(out_ref.shape[0]):
        out_ref[place] = source_ref[...]


def copies(array, count):
    return pl.pallas_call(
        copies_kernel,
        out_shape=jax.ShapeDtypeStruct((count,) + array.shape, array.dtype),
        in_specs=[VMEM],
        out_specs=VMEM,
        compiler_params=pltpu.CompilerParams(vmem_limit_bytes=LIMIT),
        name="copies",
    )(array)


def swap(array):
    pairs = [(i, i ^ 1) for i in range(lax.axis_size("layer"))]
    return lax.ppermute(array, "layer", pairs)


def shift(array, chip):
    peers = lax.axis_size("angle")
    first, last = chip * CORES * peers, (chip + 1) * CORES * peers
    return lax.ppermute(array, ("layer", "angle"), [(i, i + CORES * peers) for i in range(first, last)])


def gather(copied):
    return lax.all_to_all(copied, "angle", 0, 0)


def assemble(blocks_ref, full_ref, first_line):
    lines, width = full_ref.shape[0], blocks_ref.shape[2]
    for owner in range(blocks_ref.shape[0]):
        block = blocks_ref[owner, first_line : first_line + lines]
        full_ref[:, owner * width : (owner + 1) * width] = block


def multiply(full, weights):
    return lax.dot_general(
        full,
        weights.reshape(-1, weights.shape[2]),
        (((1,), (1,)), ((), ())),
        preferred_element_type=jnp.float32,
    )


def complex_parts(product):
    cols, rows = product.shape[0] // 2, product.shape[1] // 2
    real = product[:cols, :rows] - product[cols:, rows:]
    imag = product[cols:, :rows] + product[:cols, rows:]
    return real, imag


def load_kernel(layer, source_ref, out_ref, sem):
    copy = pltpu.make_async_copy(source_ref.at[layer], out_ref, sem)
    copy.start()
    copy.wait()


def image_kernel(layer, local_layer, kind, first, first_line, plan_ref, table_ref, weight_ref, next_ref, base_ref, blocks_ref, out_ref, *refs):
    *fetched_refs, total_ref, full_ref, weights, sems = refs
    wide, rows = total_ref.shape
    cols = wide // 2
    slots = weight_ref.shape[1]
    used = [jnp.max(plan_ref[layer, slot]) == kind for slot in range(slots)]
    copied = []
    for slot in range(slots):
        copied.append(pltpu.make_async_copy(weight_ref.at[local_layer, slot], weights.at[slot], sems.at[slot]))
        pl.when(used[slot])(copied[slot].start)
    fetches = [pltpu.make_async_copy(next_ref.at[local_layer], ref, sems.at[slots]) for ref in fetched_refs]
    for fetch in fetches:
        fetch.start()
    base = base_ref[layer] if first else base_ref[...]
    total_ref[...] = base.astype(jnp.float32)
    assemble(blocks_ref, full_ref, first_line)
    for slot in range(slots):

        @pl.when(used[slot])
        def _(slot=slot):
            copied[slot].wait()
            real, imag = complex_parts(multiply(full_ref[...], weights[slot]))
            cosine = jnp.broadcast_to(table_ref[layer, slot, 0][:, :1], (cols, rows))
            sine = jnp.broadcast_to(table_ref[layer, slot, 1][:, :1], (cols, rows))
            total_ref[:cols] -= real * cosine - imag * sine
            total_ref[cols:] -= real * sine + imag * cosine

    if out_ref.ndim == 2:
        out_ref[...] = total_ref[...]
    else:
        total = total_ref[...].astype(jnp.bfloat16)
        for place in range(out_ref.shape[0]):
            out_ref[place] = total
    for fetch in fetches:
        fetch.wait()


def inverse_kernel(parts, weight_ref, blocks_ref, field_ref, *refs):
    copied_refs, full_ref = refs[:-1], refs[-1]
    assemble(blocks_ref, full_ref, 0)
    product = multiply(full_ref[...], weight_ref[...])
    wide = product.shape[0] // parts
    pieces = []
    for part in range(parts):
        pieces += complex_parts(product[part * wide : (part + 1) * wide])
    field = jnp.concatenate(pieces).astype(jnp.bfloat16)
    field_ref[...] = field
    for copied_ref in copied_refs:
        for place in range(copied_ref.shape[0]):
            copied_ref[place] = field


def nothing(shapes):
    return list(
        pl.pallas_call(
            lambda *refs: None, out_shape=shapes, out_specs=[ANY] * len(shapes), name="nothing"
        )()
    )


def held(array):
    return pltpu.with_memory_space_constraint(array, pltpu.VMEM)


def far(array):
    return pltpu.with_memory_space_constraint(array, pltpu.HBM)


def local(right_side, inverse, coupling, image_offset, image_count, phase_exponent):
    layers, rows, _, cols = right_side.shape
    slots, unknowns = coupling.shape[1], coupling.shape[4]
    peers = lax.axis_size("angle")
    chips = lax.axis_size("layer") // CORES
    chip, core = jnp.divmod(lax.axis_index("layer"), CORES)
    deep = CORES * layers
    width = cols // CORES
    wide = 2 * width

    def ordered(mine, given):
        return jnp.where(core == 0, jnp.concatenate([mine, given]), jnp.concatenate([given, mine]))

    right = right_side.reshape(layers, rows, 2, CORES, width).transpose(3, 0, 2, 4, 1)
    split = right.reshape(CORES, layers, wide, rows)
    right = ordered(
        jnp.where(core == 0, split[0], split[1]), swap(jnp.where(core == 0, split[1], split[0]))
    )
    kinds = jnp.where(lax.iota(jnp.int32, slots) < image_count[:, None], image_offset, 0)
    both = jnp.stack([kinds, phase_exponent], 1)
    both = ordered(both, swap(both))
    begin = split[:, 0].reshape(CORES * wide, rows)
    tied = lax.optimization_barrier((right, both, begin, inverse, coupling))
    right, both, begin, late_inverse, late_coupling = tied
    other_coupling, other_inverse = swap(late_coupling), swap(late_inverse)
    plan = jnp.broadcast_to(both[:, 0].astype(jnp.float32)[..., None, None], (deep, slots, 8, 128))
    angle = ((core * width + lax.iota(jnp.int32, width)) // NRHS).astype(jnp.float32)
    phase = (2.0 * math.pi / ANGLES) * both[:, 1].astype(jnp.float32)[:, :, None] * (angle + 0.5)
    table = jnp.stack([jnp.cos(phase), jnp.sin(phase)], 2)
    table = jnp.broadcast_to(table[..., None], table.shape + (128,))

    params = pltpu.CompilerParams(vmem_limit_bytes=LIMIT)
    field_shape = jax.ShapeDtypeStruct((wide, rows), jnp.bfloat16)
    copied_shape = jax.ShapeDtypeStruct((peers, wide, rows), jnp.bfloat16)
    full_scratch = pltpu.VMEM((wide, unknowns), jnp.bfloat16)

    def cost(planes):
        return pl.CostEstimate(
            flops=4 * wide * rows * unknowns * planes,
            bytes_accessed=4 * rows * unknowns * planes,
            transcendentals=0,
        )

    def images(layer, side, kind, base, blocks):
        weights, following = (coupling, inverse) if layer // layers == side else (other_coupling, other_inverse)
        first = base.ndim == 3
        first_line = side * wide if blocks.shape[1] > wide else 0
        if kind == 1:
            out_shape = [copied_shape, pltpu.VMEM(inverse.shape[1:], inverse.dtype)]
        else:
            out_shape = [jax.ShapeDtypeStruct((wide, rows), jnp.float32)]
        return pl.pallas_call(
            functools.partial(image_kernel, layer, layer % layers, kind, first, first_line),
            out_shape=out_shape,
            in_specs=[VMEM] * 2 + [ANY] * 2 + [VMEM] * 2,
            out_specs=[VMEM] * len(out_shape),
            scratch_shapes=[
                pltpu.VMEM((wide, rows), jnp.float32),
                full_scratch,
                pltpu.VMEM((slots, 2, rows, unknowns), jnp.bfloat16),
                pltpu.SemaphoreType.DMA((slots + 1,)),
            ],
            compiler_params=params,
            cost_estimate=cost(slots // 2),
            name="images_%d" % kind,
        )(plan, table, far(weights), far(following), base, blocks)

    def invert(blocks, weights, last):
        peers, lines, _ = blocks.shape
        field = jax.ShapeDtypeStruct((lines, rows), jnp.bfloat16)
        out_shape = [field] + [jax.ShapeDtypeStruct(blocks.shape, jnp.bfloat16)] * (not last)
        return pl.pallas_call(
            functools.partial(inverse_kernel, lines // wide),
            out_shape=out_shape,
            in_specs=[VMEM] * 2,
            out_specs=[VMEM] * len(out_shape),
            scratch_shapes=[pltpu.VMEM((lines, unknowns), jnp.bfloat16)],
            compiler_params=params,
            cost_estimate=cost(1),
            name="invert",
        )(held(weights), blocks)

    def load(layer):
        return pl.pallas_call(
            functools.partial(load_kernel, layer),
            out_shape=pltpu.VMEM(inverse.shape[1:], inverse.dtype),
            in_specs=[ANY],
            out_specs=VMEM,
            scratch_shapes=[pltpu.SemaphoreType.DMA],
            compiler_params=pltpu.CompilerParams(vmem_limit_bytes=2**20),
            name="load",
        )(far(inverse))

    def run(side, start, latest, earlier):
        fields = []
        for layer in range(start, deep):
            base = right if earlier is None else images(layer, side, 2, right, earlier)[0]
            copied, weights = images(layer, side, 1, base, latest)
            field, *copied = invert(gather(copied), weights, layer + 1 == deep)
            fields.append(field)
            if copied:
                earlier, latest = latest, gather(copied[0])
        return [*fields, latest]

    def on_chip(number, shapes, functions, *operands):
        which = jnp.where(chip == number, core + 1, 0)
        return lax.switch(which, [lambda *_: nothing(shapes), *functions], *operands)

    found = []
    field = earlier = None
    for number in range(chips):
        if number == 0:
            wider = jax.ShapeDtypeStruct((CORES * wide, rows), jnp.bfloat16)
            gathered = jax.ShapeDtypeStruct((peers, CORES * wide, rows), jnp.bfloat16)

            def layer_zero(begin):
                weights = load(0)
                field, copied = invert(gather(copies(begin, peers)), weights, False)
                return [field, gather(copied)]

            shapes = [wider, gathered]
            zero, latest = on_chip(0, shapes, [layer_zero, lambda *_: nothing(shapes)], begin)
            pairs = [(b, peers + b) for b in range(peers)]
            given = lax.ppermute(latest, ("layer", "angle"), pairs)
            functions = [lambda mine, _: run(0, 1, mine, None), lambda _, given: run(1, 1, given, None)]
            operands = (latest, given)
            start = 1
        else:
            functions = [
                lambda field, earlier, side=side: run(side, 0, gather(copies(field, peers)), earlier)
                for side in range(CORES)
            ]
            operands = (field, earlier)
            start = 0
        shapes = [field_shape] * (deep - start) + [copied_shape]
        *fields, latest = on_chip(number, shapes, functions, *operands)
        found.append(([zero[:wide]] if start else []) + fields)
        if number + 1 < chips:
            field, earlier = shift(fields[-1], number), shift(latest, number)

    chosen = []
    for layer in range(deep):
        value = found[0][layer]
        for number in range(1, chips):
            value = jnp.where(chip == number, found[number][layer], value)
        chosen.append(value)
    low, high = jnp.stack(chosen[:layers]), jnp.stack(chosen[layers:])
    mine = jnp.where(core == 0, low, high)
    given = swap(jnp.where(core == 0, high, low))
    first_given = jnp.where(chip == 0, jnp.where(core == 0, zero[wide:], given[0]), given[0])
    given = jnp.concatenate([first_given[None], given[1:]])
    result = jnp.where(core == 0, jnp.stack([mine, given]), jnp.stack([given, mine]))
    result = result.reshape(CORES, layers, 2, width, rows).transpose(1, 4, 2, 0, 3)
    return result.reshape(layers, rows, 2, cols)


def solution(mesh):
    placed = (
        P("layer", "angle", None, None),
        P("layer", None, "angle", None),
        P("layer", None, None, "angle", None),
        P("layer", None),
        P("layer"),
        P("layer", None),
    )
    return jax.shard_map(
        local,
        mesh=mesh,
        in_specs=placed,
        out_specs=P("layer", "angle", None, None),
        check_vma=False,
    )
```

```python
import functools
import math

import jax
import jax.numpy as jnp
from jax import lax
from jax.experimental import pallas as pl
from jax.experimental.pallas import tpu as pltpu
from jax.sharding import PartitionSpec as P

ANGLES = 16
NRHS = 6
CORES = 2
LIMIT = 24 * 2**20

VMEM = pl.BlockSpec(memory_space=pltpu.VMEM)
ANY = pl.BlockSpec(memory_space=pl.ANY)


def copies_kernel(source_ref, out_ref):
    for place in range(out_ref.shape[0]):
        out_ref[place] = source_ref[...]


def copies(array, count):
    return pl.pallas_call(
        copies_kernel,
        out_shape=jax.ShapeDtypeStruct((count,) + array.shape, array.dtype),
        in_specs=[VMEM],
        out_specs=VMEM,
        compiler_params=pltpu.CompilerParams(vmem_limit_bytes=LIMIT),
        name="copies",
    )(array)


def swap(array):
    pairs = [(i, i ^ 1) for i in range(lax.axis_size("layer"))]
    return lax.ppermute(array, "layer", pairs)


def shift(array, chip):
    peers = lax.axis_size("angle")
    first, last = chip * CORES * peers, (chip + 1) * CORES * peers
    return lax.ppermute(array, ("layer", "angle"), [(i, i + CORES * peers) for i in range(first, last)])


def gather(copied):
    return lax.all_to_all(copied, "angle", 0, 0)


def assemble(blocks_ref, full_ref, first_line):
    lines, width = full_ref.shape[0], blocks_ref.shape[2]
    for owner in range(blocks_ref.shape[0]):
        block = blocks_ref[owner, first_line : first_line + lines]
        full_ref[:, owner * width : (owner + 1) * width] = block


def multiply(full, weights):
    return lax.dot_general(
        full,
        weights.reshape(-1, weights.shape[2]),
        (((1,), (1,)), ((), ())),
        preferred_element_type=jnp.float32,
    )


def complex_parts(product):
    cols, rows = product.shape[0] // 2, product.shape[1] // 2
    real = product[:cols, :rows] - product[cols:, rows:]
    imag = product[cols:, :rows] + product[:cols, rows:]
    return real, imag


def load_kernel(layer, plan_ref, own_ref, other_ref, _, out_ref, sem):
    layers = own_ref.shape[0]
    own = jnp.max(plan_ref[plan_ref.shape[0] - 1, 0]) == layer // layers
    mine = pltpu.make_async_copy(own_ref.at[layer % layers], out_ref, sem)
    given = pltpu.make_async_copy(other_ref.at[layer % layers], out_ref, sem)
    pl.when(own)(mine.start)
    pl.when(jnp.logical_not(own))(given.start)
    mine.wait()


def image_kernel(layer, kind, first, plan_ref, table_ref, own_ref, other_ref, base_ref, *refs):
    *blocks_refs, out_ref, total_ref, full_ref, weights, sems = refs
    wide, rows = total_ref.shape
    cols = wide // 2
    layers, slots = own_ref.shape[:2]
    core = jnp.max(plan_ref[plan_ref.shape[0] - 1, 0])
    own = core == layer // layers
    used = [jnp.max(plan_ref[layer, slot]) == kind for slot in range(slots)]
    waits = []
    for slot in range(slots):
        mine = pltpu.make_async_copy(own_ref.at[layer % layers, slot], weights.at[slot], sems.at[slot])
        given = pltpu.make_async_copy(other_ref.at[layer % layers, slot], weights.at[slot], sems.at[slot])
        pl.when(used[slot] & own)(mine.start)
        pl.when(used[slot] & jnp.logical_not(own))(given.start)
        waits.append(mine.wait)
    base = base_ref[layer] if first else base_ref[...]
    total_ref[...] = base.astype(jnp.float32)
    if len(blocks_refs) == 1:
        assemble(blocks_refs[0], full_ref, 0)
    else:
        for side, blocks_ref in enumerate(blocks_refs):
            pl.when(core == side)(functools.partial(assemble, blocks_ref, full_ref, side * wide))
    for slot in range(slots):

        @pl.when(used[slot])
        def _(slot=slot):
            waits[slot]()
            real, imag = complex_parts(multiply(full_ref[...], weights[slot]))
            cosine = jnp.broadcast_to(table_ref[layer, slot, 0][:, :1], (cols, rows))
            sine = jnp.broadcast_to(table_ref[layer, slot, 1][:, :1], (cols, rows))
            total_ref[:cols] -= real * cosine - imag * sine
            total_ref[cols:] -= real * sine + imag * cosine

    if out_ref.ndim == 2:
        out_ref[...] = total_ref[...]
    else:
        total = total_ref[...].astype(jnp.bfloat16)
        for place in range(out_ref.shape[0]):
            out_ref[place] = total


def inverse_kernel(parts, weight_ref, blocks_ref, field_ref, *refs):
    copied_refs, full_ref = refs[:-1], refs[-1]
    assemble(blocks_ref, full_ref, 0)
    product = multiply(full_ref[...], weight_ref[...])
    wide = product.shape[0] // parts
    pieces = []
    for part in range(parts):
        pieces += complex_parts(product[part * wide : (part + 1) * wide])
    field = jnp.concatenate(pieces).astype(jnp.bfloat16)
    field_ref[...] = field
    for copied_ref in copied_refs:
        for place in range(copied_ref.shape[0]):
            copied_ref[place] = field


def nothing(shapes):
    return list(
        pl.pallas_call(
            lambda *refs: None, out_shape=shapes, out_specs=[ANY] * len(shapes), name="nothing"
        )()
    )


def held(array):
    return pltpu.with_memory_space_constraint(array, pltpu.VMEM)


def far(array):
    return pltpu.with_memory_space_constraint(array, pltpu.HBM)


def local(right_side, inverse, coupling, image_offset, image_count, phase_exponent):
    layers, rows, _, cols = right_side.shape
    slots, unknowns = coupling.shape[1], coupling.shape[4]
    peers = lax.axis_size("angle")
    chips = lax.axis_size("layer") // CORES
    chip, core = jnp.divmod(lax.axis_index("layer"), CORES)
    deep = CORES * layers
    width = cols // CORES
    wide = 2 * width

    def ordered(mine, given):
        return jnp.where(core == 0, jnp.concatenate([mine, given]), jnp.concatenate([given, mine]))

    right = right_side.reshape(layers, rows, 2, CORES, width).transpose(3, 0, 2, 4, 1)
    split = right.reshape(CORES, layers, wide, rows)
    right = ordered(
        jnp.where(core == 0, split[0], split[1]), swap(jnp.where(core == 0, split[1], split[0]))
    )
    kinds = jnp.where(lax.iota(jnp.int32, slots) < image_count[:, None], image_offset, 0)
    both = jnp.stack([kinds, phase_exponent], 1)
    both = ordered(both, swap(both))
    begin = split[:, 0].reshape(CORES * wide, rows)
    tied = lax.optimization_barrier((right, both, begin, inverse, coupling))
    right, both, begin, late_inverse, late_coupling = tied
    other_coupling, other_inverse = swap(late_coupling), swap(late_inverse)
    plan = jnp.concatenate([both[:, 0], jnp.full((1, slots), core, jnp.int32)]).astype(jnp.float32)
    plan = jnp.broadcast_to(plan[..., None, None], (deep + 1, slots, 8, 128))
    angle = ((core * width + lax.iota(jnp.int32, width)) // NRHS).astype(jnp.float32)
    phase = (2.0 * math.pi / ANGLES) * both[:, 1].astype(jnp.float32)[:, :, None] * (angle + 0.5)
    table = jnp.stack([jnp.cos(phase), jnp.sin(phase)], 2)
    table = jnp.broadcast_to(table[..., None], table.shape + (128,))

    params = pltpu.CompilerParams(vmem_limit_bytes=LIMIT)
    field_shape = jax.ShapeDtypeStruct((wide, rows), jnp.bfloat16)
    copied_shape = jax.ShapeDtypeStruct((peers, wide, rows), jnp.bfloat16)
    full_scratch = pltpu.VMEM((wide, unknowns), jnp.bfloat16)

    def cost(planes):
        return pl.CostEstimate(
            flops=4 * wide * rows * unknowns * planes,
            bytes_accessed=4 * rows * unknowns * planes,
            transcendentals=0,
        )

    def images(layer, kind, base, blocks):
        return pl.pallas_call(
            functools.partial(image_kernel, layer, kind, base.ndim == 3),
            out_shape=copied_shape if kind == 1 else jax.ShapeDtypeStruct((wide, rows), jnp.float32),
            in_specs=[VMEM] * 2 + [ANY] * 2 + [VMEM] * (1 + len(blocks)),
            out_specs=VMEM,
            scratch_shapes=[
                pltpu.VMEM((wide, rows), jnp.float32),
                full_scratch,
                pltpu.VMEM((slots, 2, rows, unknowns), jnp.bfloat16),
                pltpu.SemaphoreType.DMA((slots,)),
            ],
            compiler_params=params,
            cost_estimate=cost(slots // 2),
            name="images_%d" % kind,
        )(plan, table, far(coupling), far(other_coupling), base, *blocks)

    def invert(blocks, weights, last):
        peers, lines, _ = blocks.shape
        field = jax.ShapeDtypeStruct((lines, rows), jnp.bfloat16)
        out_shape = [field] + [jax.ShapeDtypeStruct(blocks.shape, jnp.bfloat16)] * (not last)
        return pl.pallas_call(
            functools.partial(inverse_kernel, lines // wide),
            out_shape=out_shape,
            in_specs=[VMEM] * 2,
            out_specs=[VMEM] * len(out_shape),
            scratch_shapes=[pltpu.VMEM((lines, unknowns), jnp.bfloat16)],
            compiler_params=params,
            cost_estimate=cost(1),
            name="invert",
        )(held(weights), blocks)

    def load(layer, other, after):
        return pl.pallas_call(
            functools.partial(load_kernel, layer),
            out_shape=pltpu.VMEM(inverse.shape[1:], inverse.dtype),
            in_specs=[VMEM] + [ANY] * 3,
            out_specs=VMEM,
            scratch_shapes=[pltpu.SemaphoreType.DMA],
            compiler_params=pltpu.CompilerParams(vmem_limit_bytes=2**20),
            cost_estimate=pl.CostEstimate(flops=0, bytes_accessed=inverse.size * 2, transcendentals=0),
            name="load",
        )(plan, far(inverse), far(other), after)

    def run(start, latest, earlier):
        fields = []
        for layer in range(start, deep):
            base = right if earlier is None else images(layer, 2, right, earlier)
            copied = images(layer, 1, base, latest)
            field, *copied = invert(gather(copied), load(layer, other_inverse, copied), layer + 1 == deep)
            fields.append(field)
            if copied:
                earlier, latest = latest, [gather(copied[0])]
        return [*fields, *latest]

    def only(here, shapes, function, *operands):
        return lax.cond(here, function, lambda *_: nothing(shapes), *operands)

    found = []
    field = earlier = None
    for number in range(chips):
        if number == 0:
            wider = jax.ShapeDtypeStruct((CORES * wide, rows), jnp.bfloat16)
            gathered = jax.ShapeDtypeStruct((peers, CORES * wide, rows), jnp.bfloat16)

            def layer_zero(begin):
                copied = copies(begin, peers)
                field, copied = invert(gather(copied), load(0, inverse, copied), False)
                return [field, gather(copied)]

            shapes = [wider, gathered]
            zero, latest = only((chip == 0) & (core == 0), shapes, layer_zero, begin)
            pairs = [(b, peers + b) for b in range(peers)]
            given = lax.ppermute(latest, ("layer", "angle"), pairs)
            start, function, operands = 1, lambda *latest: run(1, latest, None), (latest, given)
        else:

            def function(field, earlier):
                return run(0, [gather(copies(field, peers))], [earlier])

            start, operands = 0, (field, earlier)
        shapes = [field_shape] * (deep - start) + [copied_shape]
        *fields, latest = only(chip == number, shapes, function, *operands)
        found.append(([zero[:wide]] if start else []) + fields)
        if number + 1 < chips:
            field, earlier = shift(fields[-1], number), shift(latest, number)

    chosen = []
    for layer in range(deep):
        value = found[0][layer]
        for number in range(1, chips):
            value = jnp.where(chip == number, found[number][layer], value)
        chosen.append(value)
    low, high = jnp.stack(chosen[:layers]), jnp.stack(chosen[layers:])
    mine = jnp.where(core == 0, low, high)
    given = swap(jnp.where(core == 0, high, low))
    first_given = jnp.where(chip == 0, jnp.where(core == 0, zero[wide:], given[0]), given[0])
    given = jnp.concatenate([first_given[None], given[1:]])
    result = jnp.where(core == 0, jnp.stack([mine, given]), jnp.stack([given, mine]))
    result = result.reshape(CORES, layers, 2, width, rows).transpose(1, 4, 2, 0, 3)
    return result.reshape(layers, rows, 2, cols)


def solution(mesh):
    placed = (
        P("layer", "angle", None, None),
        P("layer", None, "angle", None),
        P("layer", None, None, "angle", None),
        P("layer", None),
        P("layer"),
        P("layer", None),
    )
    return jax.shard_map(
        local,
        mesh=mesh,
        in_specs=placed,
        out_specs=P("layer", "angle", None, None),
        check_vma=False,
    )
```

```python
import functools
import math

import jax
import jax.numpy as jnp
from jax import lax
from jax.experimental import pallas as pl
from jax.experimental.pallas import tpu as pltpu
from jax.sharding import PartitionSpec as P

ANGLES = 16
NRHS = 6
CORES = 2
LIMIT = 24 * 2**20

VMEM = pl.BlockSpec(memory_space=pltpu.VMEM)
ANY = pl.BlockSpec(memory_space=pl.ANY)


def copies_kernel(source_ref, out_ref):
    for place in range(out_ref.shape[0]):
        out_ref[place] = source_ref[...]


def copies(array, count):
    return pl.pallas_call(
        copies_kernel,
        out_shape=jax.ShapeDtypeStruct((count,) + array.shape, array.dtype),
        in_specs=[VMEM],
        out_specs=VMEM,
        compiler_params=pltpu.CompilerParams(vmem_limit_bytes=LIMIT),
        name="copies",
    )(array)


def swap(array):
    pairs = [(i, i ^ 1) for i in range(lax.axis_size("layer"))]
    return lax.ppermute(array, "layer", pairs)


def shift(array, chip):
    peers = lax.axis_size("angle")
    first, last = chip * CORES * peers, (chip + 1) * CORES * peers
    return lax.ppermute(array, ("layer", "angle"), [(i, i + CORES * peers) for i in range(first, last)])


def gather(copied):
    return lax.all_to_all(copied, "angle", 0, 0)


def assemble(blocks_ref, full_ref, first_line):
    lines, width = full_ref.shape[0], blocks_ref.shape[2]
    for owner in range(blocks_ref.shape[0]):
        block = blocks_ref[owner, first_line : first_line + lines]
        full_ref[:, owner * width : (owner + 1) * width] = block


def multiply(full, weights):
    return lax.dot_general(
        full,
        weights.reshape(-1, weights.shape[2]),
        (((1,), (1,)), ((), ())),
        preferred_element_type=jnp.float32,
    )


def complex_parts(product):
    cols, rows = product.shape[0] // 2, product.shape[1] // 2
    real = product[:cols, :rows] - product[cols:, rows:]
    imag = product[cols:, :rows] + product[:cols, rows:]
    return real, imag


def load_kernel(layer, plan_ref, own_ref, other_ref, _, out_ref, sem):
    layers = own_ref.shape[0]
    own = jnp.max(plan_ref[plan_ref.shape[0] - 1, 0]) == layer // layers
    mine = pltpu.make_async_copy(own_ref.at[layer % layers], out_ref, sem)
    given = pltpu.make_async_copy(other_ref.at[layer % layers], out_ref, sem)
    pl.when(own)(mine.start)
    pl.when(jnp.logical_not(own))(given.start)
    mine.wait()


def image_kernel(layer, kind, first, plan_ref, table_ref, own_ref, other_ref, base_ref, *refs):
    *blocks_refs, out_ref, total_ref, full_ref, weights, sems = refs
    wide, rows = total_ref.shape
    cols = wide // 2
    layers, slots = own_ref.shape[:2]
    core = jnp.max(plan_ref[plan_ref.shape[0] - 1, 0])
    used = [jnp.max(plan_ref[layer, slot]) == kind for slot in range(slots)]

    def body(weight_ref):
        copied = []
        for slot in range(slots):
            source = weight_ref.at[layer % layers, slot]
            copied.append(pltpu.make_async_copy(source, weights.at[slot], sems.at[slot]))
            pl.when(used[slot])(copied[slot].start)
        base = base_ref[layer] if first else base_ref[...]
        total_ref[...] = base.astype(jnp.float32)
        if len(blocks_refs) == 1:
            assemble(blocks_refs[0], full_ref, 0)
        else:
            for side, blocks_ref in enumerate(blocks_refs):
                pl.when(core == side)(functools.partial(assemble, blocks_ref, full_ref, side * wide))
        for slot in range(slots):

            @pl.when(used[slot])
            def _(slot=slot):
                copied[slot].wait()
                real, imag = complex_parts(multiply(full_ref[...], weights[slot]))
                cosine = jnp.broadcast_to(table_ref[layer, slot, 0][:, :1], (cols, rows))
                sine = jnp.broadcast_to(table_ref[layer, slot, 1][:, :1], (cols, rows))
                total_ref[:cols] -= real * cosine - imag * sine
                total_ref[cols:] -= real * sine + imag * cosine

    pl.when(core == layer // layers)(functools.partial(body, own_ref))
    pl.when(core != layer // layers)(functools.partial(body, other_ref))
    if out_ref.ndim == 2:
        out_ref[...] = total_ref[...]
    else:
        total = total_ref[...].astype(jnp.bfloat16)
        for place in range(out_ref.shape[0]):
            out_ref[place] = total


def inverse_kernel(parts, weight_ref, blocks_ref, *refs):
    field_refs, copied_refs, full_ref = refs[:parts], refs[parts:-1], refs[-1]
    assemble(blocks_ref, full_ref, 0)
    product = multiply(full_ref[...], weight_ref[...])
    wide = product.shape[0] // parts
    for part, field_ref in enumerate(field_refs):
        pieces = complex_parts(product[part * wide : (part + 1) * wide])
        field = jnp.concatenate(pieces).astype(jnp.bfloat16)
        field_ref[...] = field
        for copied_ref in copied_refs:
            for place in range(copied_ref.shape[0]):
                copied_ref[place, part * wide : (part + 1) * wide] = field


def nothing(shapes):
    return list(
        pl.pallas_call(
            lambda *refs: None, out_shape=shapes, out_specs=[ANY] * len(shapes), name="nothing"
        )()
    )


def held(array):
    return pltpu.with_memory_space_constraint(array, pltpu.VMEM)


def far(array):
    return pltpu.with_memory_space_constraint(array, pltpu.HBM)


def local(right_side, inverse, coupling, image_offset, image_count, phase_exponent):
    layers, rows, _, cols = right_side.shape
    slots, unknowns = coupling.shape[1], coupling.shape[4]
    peers = lax.axis_size("angle")
    chips = lax.axis_size("layer") // CORES
    chip, core = jnp.divmod(lax.axis_index("layer"), CORES)
    deep = CORES * layers
    width = cols // CORES
    wide = 2 * width

    def ordered(mine, given):
        return jnp.where(core == 0, jnp.concatenate([mine, given]), jnp.concatenate([given, mine]))

    right = right_side.reshape(layers, rows, 2, CORES, width).transpose(3, 0, 2, 4, 1)
    split = right.reshape(CORES, layers, wide, rows)
    right = ordered(
        jnp.where(core == 0, split[0], split[1]), swap(jnp.where(core == 0, split[1], split[0]))
    )
    kinds = jnp.where(lax.iota(jnp.int32, slots) < image_count[:, None], image_offset, 0)
    both = jnp.stack([kinds, phase_exponent], 1)
    both = ordered(both, swap(both))
    begin = split[:, 0].reshape(CORES * wide, rows)
    tied = lax.optimization_barrier((right, both, begin, inverse, coupling))
    right, both, begin, late_inverse, late_coupling = tied
    other_coupling, other_inverse = swap(late_coupling), swap(late_inverse)
    plan = jnp.concatenate([both[:, 0], jnp.full((1, slots), core, jnp.int32)]).astype(jnp.float32)
    plan = jnp.broadcast_to(plan[..., None, None], (deep + 1, slots, 8, 128))
    angle = ((core * width + lax.iota(jnp.int32, width)) // NRHS).astype(jnp.float32)
    phase = (2.0 * math.pi / ANGLES) * both[:, 1].astype(jnp.float32)[:, :, None] * (angle + 0.5)
    table = jnp.stack([jnp.cos(phase), jnp.sin(phase)], 2)
    table = jnp.broadcast_to(table[..., None], table.shape + (128,))

    params = pltpu.CompilerParams(vmem_limit_bytes=LIMIT)
    field_shape = jax.ShapeDtypeStruct((wide, rows), jnp.bfloat16)
    copied_shape = jax.ShapeDtypeStruct((peers, wide, rows), jnp.bfloat16)
    full_scratch = pltpu.VMEM((wide, unknowns), jnp.bfloat16)

    def cost(planes):
        return pl.CostEstimate(
            flops=4 * wide * rows * unknowns * planes,
            bytes_accessed=4 * rows * unknowns * planes,
            transcendentals=0,
        )

    def images(layer, kind, base, blocks):
        return pl.pallas_call(
            functools.partial(image_kernel, layer, kind, base.ndim == 3),
            out_shape=copied_shape if kind == 1 else jax.ShapeDtypeStruct((wide, rows), jnp.float32),
            in_specs=[VMEM] * 2 + [ANY] * 2 + [VMEM] * (1 + len(blocks)),
            out_specs=VMEM,
            scratch_shapes=[
                pltpu.VMEM((wide, rows), jnp.float32),
                full_scratch,
                pltpu.VMEM((slots, 2, rows, unknowns), jnp.bfloat16),
                pltpu.SemaphoreType.DMA((slots,)),
            ],
            compiler_params=params,
            cost_estimate=cost(slots // 2),
            name="images_%d" % kind,
        )(plan, table, far(coupling), far(other_coupling), base, *blocks)

    def invert(blocks, weights, last):
        parts = blocks.shape[1] // wide
        out_shape = [field_shape] * parts + [jax.ShapeDtypeStruct(blocks.shape, jnp.bfloat16)] * (not last)
        return pl.pallas_call(
            functools.partial(inverse_kernel, parts),
            out_shape=out_shape,
            in_specs=[VMEM] * 2,
            out_specs=[VMEM] * len(out_shape),
            scratch_shapes=[pltpu.VMEM((parts * wide, unknowns), jnp.bfloat16)],
            compiler_params=params,
            cost_estimate=cost(1),
            name="invert",
        )(held(weights), blocks)

    def load(layer, other, after):
        return pl.pallas_call(
            functools.partial(load_kernel, layer),
            out_shape=pltpu.VMEM(inverse.shape[1:], inverse.dtype),
            in_specs=[VMEM] + [ANY] * 3,
            out_specs=VMEM,
            scratch_shapes=[pltpu.SemaphoreType.DMA],
            compiler_params=pltpu.CompilerParams(vmem_limit_bytes=2**20),
            cost_estimate=pl.CostEstimate(flops=0, bytes_accessed=inverse.size * 2, transcendentals=0),
            name="load",
        )(plan, far(inverse), far(other), after)

    def run(start, latest, earlier):
        fields = []
        for layer in range(start, deep):
            base = right if earlier is None else images(layer, 2, right, earlier)
            copied = images(layer, 1, base, latest)
            if layer + 1 < deep:
                field, next_copied = invert(gather(copied), load(layer, other_inverse, copied), False)
                fields.append(field)
                earlier, latest = latest, [gather(next_copied)]
        return [*fields, copied, *latest]

    def finish(copied):
        return list(invert(gather(copied), load(deep - 1, other_inverse, copied), True))

    def only(here, shapes, function, *operands):
        return lax.cond(here, function, lambda *_: nothing(shapes), *operands)

    found = []
    field = earlier = None
    for number in range(chips):
        if number == 0:
            gathered = jax.ShapeDtypeStruct((peers, CORES * wide, rows), jnp.bfloat16)

            def layer_zero(begin):
                copied = copies(begin, peers)
                *fields, copied = invert(gather(copied), load(0, inverse, copied), False)
                return [*fields, gather(copied)]

            shapes = [field_shape] * CORES + [gathered]
            *zero, latest = only((chip == 0) & (core == 0), shapes, layer_zero, begin)
            pairs = [(b, peers + b) for b in range(peers)]
            given = lax.ppermute(latest, ("layer", "angle"), pairs)
            start, function, operands = 1, lambda *latest: run(1, latest, None), (latest, given)
        else:

            def function(field, earlier):
                return run(0, [gather(copies(field, peers))], [earlier])

            start, operands = 0, (field, earlier)
        here = chip == number
        shapes = [field_shape] * (deep - start - 1) + [copied_shape] * 2
        *fields, copied, latest = only(here, shapes, function, *operands)
        if number + 1 < chips:
            earlier = shift(latest, number)
        (last,) = only(here, [field_shape], finish, copied)
        found.append((zero[:1] if start else []) + fields + [last])
        if number + 1 < chips:
            field = shift(last, number)

    chosen = []
    for layer in range(deep):
        value = found[0][layer]
        for number in range(1, chips):
            value = jnp.where(chip == number, found[number][layer], value)
        chosen.append(value)
    low, high = jnp.stack(chosen[:layers]), jnp.stack(chosen[layers:])
    mine = jnp.where(core == 0, low, high)
    given = swap(jnp.where(core == 0, high, low))
    first_given = jnp.where(chip == 0, jnp.where(core == 0, zero[1], given[0]), given[0])
    given = jnp.concatenate([first_given[None], given[1:]])
    result = jnp.where(core == 0, jnp.stack([mine, given]), jnp.stack([given, mine]))
    result = result.reshape(CORES, layers, 2, width, rows).transpose(1, 4, 2, 0, 3)
    return result.reshape(layers, rows, 2, cols)


def solution(mesh):
    placed = (
        P("layer", "angle", None, None),
        P("layer", None, "angle", None),
        P("layer", None, None, "angle", None),
        P("layer", None),
        P("layer"),
        P("layer", None),
    )
    return jax.shard_map(
        local,
        mesh=mesh,
        in_specs=placed,
        out_specs=P("layer", "angle", None, None),
        check_vma=False,
    )
```

```python
import functools
import math

import jax
import jax.numpy as jnp
from jax import lax
from jax.experimental import pallas as pl
from jax.experimental.pallas import tpu as pltpu
from jax.sharding import PartitionSpec as P

ANGLES = 16
NRHS = 6
CORES = 2
LIMIT = 24 * 2**20

VMEM = pl.BlockSpec(memory_space=pltpu.VMEM)
ANY = pl.BlockSpec(memory_space=pl.ANY)


def copies_kernel(source_ref, out_ref):
    for place in range(out_ref.shape[0]):
        out_ref[place] = source_ref[...]


def copies(array, count):
    return pl.pallas_call(
        copies_kernel,
        out_shape=jax.ShapeDtypeStruct((count,) + array.shape, array.dtype),
        in_specs=[VMEM],
        out_specs=VMEM,
        compiler_params=pltpu.CompilerParams(vmem_limit_bytes=LIMIT),
        name="copies",
    )(array)


def swap(array):
    pairs = [(i, i ^ 1) for i in range(lax.axis_size("layer"))]
    return lax.ppermute(array, "layer", pairs)


def shift(array, chip):
    peers = lax.axis_size("angle")
    first, last = chip * CORES * peers, (chip + 1) * CORES * peers
    return lax.ppermute(array, ("layer", "angle"), [(i, i + CORES * peers) for i in range(first, last)])


def gather(copied):
    return lax.all_to_all(copied, "angle", 0, 0)


def assemble(blocks_ref, full_ref, first_line):
    lines, width = full_ref.shape[0], blocks_ref.shape[2]
    for owner in range(blocks_ref.shape[0]):
        block = blocks_ref[owner, first_line : first_line + lines]
        full_ref[:, owner * width : (owner + 1) * width] = block


def multiply(full, weights):
    return lax.dot_general(
        full,
        weights.reshape(-1, weights.shape[2]),
        (((1,), (1,)), ((), ())),
        preferred_element_type=jnp.float32,
    )


def complex_parts(product):
    cols, rows = product.shape[0] // 2, product.shape[1] // 2
    real = product[:cols, :rows] - product[cols:, rows:]
    imag = product[cols:, :rows] + product[:cols, rows:]
    return real, imag


def load_kernel(layer, plan_ref, own_ref, other_ref, _, out_ref, sem):
    layers = own_ref.shape[0]
    own = jnp.max(plan_ref[plan_ref.shape[0] - 1, 0]) == layer // layers
    mine = pltpu.make_async_copy(own_ref.at[layer % layers], out_ref, sem)
    given = pltpu.make_async_copy(other_ref.at[layer % layers], out_ref, sem)
    pl.when(own)(mine.start)
    pl.when(jnp.logical_not(own))(given.start)
    mine.wait()


def image_kernel(layer, kind, first, ready, plan_ref, table_ref, own_ref, other_ref, base_ref, *refs):
    *blocks_refs, out_ref, total_ref, full_ref, weights, sems = refs
    ready_ref = blocks_refs.pop() if ready else None
    wide, rows = total_ref.shape
    cols = wide // 2
    layers, slots = own_ref.shape[:2]
    core = jnp.max(plan_ref[plan_ref.shape[0] - 1, 0])
    used = [jnp.max(plan_ref[layer, slot]) == kind for slot in range(slots)]

    def body(weight_ref):
        copied = []
        for slot in range(slots):
            source = weight_ref.at[layer % layers, slot]
            copied.append(pltpu.make_async_copy(source, weights.at[slot], sems.at[slot]))
            pl.when(used[slot])(copied[slot].start)
        base = base_ref[layer] if first else base_ref[...]
        total_ref[...] = base.astype(jnp.float32)
        if len(blocks_refs) == 1:
            assemble(blocks_refs[0], full_ref, 0)
        else:
            for side, blocks_ref in enumerate(blocks_refs):
                pl.when(core == side)(functools.partial(assemble, blocks_ref, full_ref, side * wide))
        for slot in range(slots):

            @pl.when(used[slot])
            def _(slot=slot):
                copied[slot].wait()
                real, imag = complex_parts(multiply(full_ref[...], weights[slot]))
                cosine = jnp.broadcast_to(table_ref[layer, slot, 0][:, :1], (cols, rows))
                sine = jnp.broadcast_to(table_ref[layer, slot, 1][:, :1], (cols, rows))
                total_ref[:cols] -= real * cosine - imag * sine
                total_ref[cols:] -= real * sine + imag * cosine

    if not ready:
        pl.when(core == layer // layers)(functools.partial(body, own_ref))
    pl.when(core != layer // layers)(functools.partial(body, other_ref))
    if out_ref.ndim == 2:
        out_ref[...] = total_ref[...]
    else:
        total = total_ref[...].astype(jnp.bfloat16)
        if ready:
            total = jnp.where(core == layer // layers, ready_ref[0], total)
        for place in range(out_ref.shape[0]):
            out_ref[place] = total


def inverse_kernel(parts, weight_ref, blocks_ref, *refs):
    field_refs, copied_refs, full_ref = refs[:parts], refs[parts:-1], refs[-1]
    assemble(blocks_ref, full_ref, 0)
    product = multiply(full_ref[...], weight_ref[...])
    wide = product.shape[0] // parts
    for part, field_ref in enumerate(field_refs):
        pieces = complex_parts(product[part * wide : (part + 1) * wide])
        field = jnp.concatenate(pieces).astype(jnp.bfloat16)
        field_ref[...] = field
        for copied_ref in copied_refs:
            for place in range(copied_ref.shape[0]):
                copied_ref[place, part * wide : (part + 1) * wide] = field


def nothing(shapes):
    return list(
        pl.pallas_call(
            lambda *refs: None, out_shape=shapes, out_specs=[ANY] * len(shapes), name="nothing"
        )()
    )


def held(array):
    return pltpu.with_memory_space_constraint(array, pltpu.VMEM)


def far(array):
    return pltpu.with_memory_space_constraint(array, pltpu.HBM)


def local(right_side, inverse, coupling, image_offset, image_count, phase_exponent):
    layers, rows, _, cols = right_side.shape
    slots, unknowns = coupling.shape[1], coupling.shape[4]
    peers = lax.axis_size("angle")
    chips = lax.axis_size("layer") // CORES
    chip, core = jnp.divmod(lax.axis_index("layer"), CORES)
    deep = CORES * layers
    width = cols // CORES
    wide = 2 * width

    def ordered(mine, given):
        return jnp.where(core == 0, jnp.concatenate([mine, given]), jnp.concatenate([given, mine]))

    right = right_side.reshape(layers, rows, 2, CORES, width).transpose(3, 0, 2, 4, 1)
    split = right.reshape(CORES, layers, wide, rows)
    right = ordered(
        jnp.where(core == 0, split[0], split[1]), swap(jnp.where(core == 0, split[1], split[0]))
    )
    kinds = jnp.where(lax.iota(jnp.int32, slots) < image_count[:, None], image_offset, 0)
    both = jnp.stack([kinds, phase_exponent], 1)
    both = ordered(both, swap(both))
    begin = split[:, 0].reshape(CORES * wide, rows)
    tied = lax.optimization_barrier((right, both, begin, inverse, coupling))
    right, both, begin, late_inverse, late_coupling = tied
    other_coupling, other_inverse = swap(late_coupling), swap(late_inverse)
    plan = jnp.concatenate([both[:, 0], jnp.full((1, slots), core, jnp.int32)]).astype(jnp.float32)
    plan = jnp.broadcast_to(plan[..., None, None], (deep + 1, slots, 8, 128))
    angle = ((core * width + lax.iota(jnp.int32, width)) // NRHS).astype(jnp.float32)
    phase = (2.0 * math.pi / ANGLES) * both[:, 1].astype(jnp.float32)[:, :, None] * (angle + 0.5)
    table = jnp.stack([jnp.cos(phase), jnp.sin(phase)], 2)
    table = jnp.broadcast_to(table[..., None], table.shape + (128,))

    params = pltpu.CompilerParams(vmem_limit_bytes=LIMIT)
    field_shape = jax.ShapeDtypeStruct((wide, rows), jnp.bfloat16)
    copied_shape = jax.ShapeDtypeStruct((peers, wide, rows), jnp.bfloat16)
    full_scratch = pltpu.VMEM((wide, unknowns), jnp.bfloat16)

    def cost(planes):
        return pl.CostEstimate(
            flops=4 * wide * rows * unknowns * planes,
            bytes_accessed=4 * rows * unknowns * planes,
            transcendentals=0,
        )

    def images(layer, kind, base, blocks, other=None, ready=None):
        blocks = blocks if ready is None else [*blocks, ready]
        return pl.pallas_call(
            functools.partial(image_kernel, layer, kind, base.ndim == 3, ready is not None),
            out_shape=copied_shape if kind == 1 else jax.ShapeDtypeStruct((wide, rows), jnp.float32),
            in_specs=[VMEM] * 2 + [ANY] * 2 + [VMEM] * (1 + len(blocks)),
            out_specs=VMEM,
            scratch_shapes=[
                pltpu.VMEM((wide, rows), jnp.float32),
                full_scratch,
                pltpu.VMEM((slots, 2, rows, unknowns), jnp.bfloat16),
                pltpu.SemaphoreType.DMA((slots,)),
            ],
            compiler_params=params,
            cost_estimate=cost(slots // 2),
            name="images_%d" % kind,
        )(plan, table, far(coupling), far(other_coupling if other is None else other), base, *blocks)

    def invert(blocks, weights, last):
        parts = blocks.shape[1] // wide
        out_shape = [field_shape] * parts + [jax.ShapeDtypeStruct(blocks.shape, jnp.bfloat16)] * (not last)
        return pl.pallas_call(
            functools.partial(inverse_kernel, parts),
            out_shape=out_shape,
            in_specs=[VMEM] * 2,
            out_specs=[VMEM] * len(out_shape),
            scratch_shapes=[pltpu.VMEM((parts * wide, unknowns), jnp.bfloat16)],
            compiler_params=params,
            cost_estimate=cost(1),
            name="invert",
        )(held(weights), blocks)

    def load(layer, other, after):
        return pl.pallas_call(
            functools.partial(load_kernel, layer),
            out_shape=pltpu.VMEM(inverse.shape[1:], inverse.dtype),
            in_specs=[VMEM] + [ANY] * 3,
            out_specs=VMEM,
            scratch_shapes=[pltpu.SemaphoreType.DMA],
            compiler_params=pltpu.CompilerParams(vmem_limit_bytes=2**20),
            cost_estimate=pl.CostEstimate(flops=0, bytes_accessed=inverse.size * 2, transcendentals=0),
            name="load",
        )(plan, far(inverse), far(other), after)

    def run(start, latest, earlier, ready=None):
        fields = []
        for layer in range(start, deep):
            base = right if earlier is None else images(layer, 2, right, earlier)
            copied = images(layer, 1, base, latest, ready=ready if layer == start else None)
            if layer + 1 < deep:
                field, next_copied = invert(gather(copied), load(layer, other_inverse, copied), False)
                fields.append(field)
                earlier, latest = latest, [gather(next_copied)]
        return [*fields, copied, *latest]

    def finish(copied):
        return list(invert(gather(copied), load(deep - 1, other_inverse, copied), True))

    def only(here, shapes, function, *operands):
        return lax.cond(here, function, lambda *_: nothing(shapes), *operands)

    found = []
    field = earlier = None
    for number in range(chips):
        if number == 0:
            gathered = jax.ShapeDtypeStruct((peers, CORES * wide, rows), jnp.bfloat16)

            def layer_zero(begin):
                copied = copies(begin, peers)
                *fields, copied = invert(gather(copied), load(0, inverse, copied), False)
                latest = gather(copied)
                return [*fields, latest, images(1, 1, right, [latest], other=coupling)]

            shapes = [field_shape] * CORES + [gathered, copied_shape]
            *zero, latest, ready = only((chip == 0) & (core == 0), shapes, layer_zero, begin)
            pairs = [(b, peers + b) for b in range(peers)]
            given = lax.ppermute(latest, ("layer", "angle"), pairs)
            start, function, operands = 1, lambda ready, *latest: run(1, latest, None, ready), (ready, latest, given)
        else:

            def function(field, earlier):
                return run(0, [gather(copies(field, peers))], [earlier])

            start, operands = 0, (field, earlier)
        here = chip == number
        shapes = [field_shape] * (deep - start - 1) + [copied_shape] * 2
        *fields, copied, latest = only(here, shapes, function, *operands)
        if number + 1 < chips:
            earlier = shift(latest, number)
        (last,) = only(here, [field_shape], finish, copied)
        found.append((zero[:1] if start else []) + fields + [last])
        if number + 1 < chips:
            field = shift(last, number)

    chosen = []
    for layer in range(deep):
        value = found[0][layer]
        for number in range(1, chips):
            value = jnp.where(chip == number, found[number][layer], value)
        chosen.append(value)
    low, high = jnp.stack(chosen[:layers]), jnp.stack(chosen[layers:])
    mine = jnp.where(core == 0, low, high)
    given = swap(jnp.where(core == 0, high, low))
    first_given = jnp.where(chip == 0, jnp.where(core == 0, zero[1], given[0]), given[0])
    given = jnp.concatenate([first_given[None], given[1:]])
    result = jnp.where(core == 0, jnp.stack([mine, given]), jnp.stack([given, mine]))
    result = result.reshape(CORES, layers, 2, width, rows).transpose(1, 4, 2, 0, 3)
    return result.reshape(layers, rows, 2, cols)


def solution(mesh):
    placed = (
        P("layer", "angle", None, None),
        P("layer", None, "angle", None),
        P("layer", None, None, "angle", None),
        P("layer", None),
        P("layer"),
        P("layer", None),
    )
    return jax.shard_map(
        local,
        mesh=mesh,
        in_specs=placed,
        out_specs=P("layer", "angle", None, None),
        check_vma=False,
    )
```

```python
import functools
import math

import jax
import jax.numpy as jnp
from jax import lax
from jax.experimental import pallas as pl
from jax.experimental.pallas import tpu as pltpu
from jax.sharding import PartitionSpec as P

ANGLES = 16
NRHS = 6
CORES = 2
LIMIT = 24 * 2**20

VMEM = pl.BlockSpec(memory_space=pltpu.VMEM)
ANY = pl.BlockSpec(memory_space=pl.ANY)


def copies_kernel(source_ref, out_ref):
    for place in range(out_ref.shape[0]):
        out_ref[place] = source_ref[...]


def copies(array, count):
    return pl.pallas_call(
        copies_kernel,
        out_shape=jax.ShapeDtypeStruct((count,) + array.shape, array.dtype),
        in_specs=[VMEM],
        out_specs=VMEM,
        compiler_params=pltpu.CompilerParams(vmem_limit_bytes=LIMIT),
        name="copies",
    )(array)


def swap(array):
    pairs = [(i, i ^ 1) for i in range(lax.axis_size("layer"))]
    return lax.ppermute(array, "layer", pairs)


def shift(array, chip):
    peers = lax.axis_size("angle")
    first, last = chip * CORES * peers, (chip + 1) * CORES * peers
    return lax.ppermute(array, ("layer", "angle"), [(i, i + CORES * peers) for i in range(first, last)])


def gather(copied):
    return lax.all_to_all(copied, "angle", 0, 0)


def assemble(blocks_ref, full_ref, side):
    lines, width = full_ref.shape[0], blocks_ref.shape[2]
    half, whole = lines // 2, blocks_ref.shape[1] // 2
    for owner in range(blocks_ref.shape[0]):
        columns = slice(owner * width, (owner + 1) * width)
        for part in range(2):
            first = part * whole + side * half
            full_ref[part * half : (part + 1) * half, columns] = blocks_ref[owner, first : first + half]


def multiply(full, weights):
    return lax.dot_general(
        full,
        weights.reshape(-1, weights.shape[2]),
        (((1,), (1,)), ((), ())),
        preferred_element_type=jnp.float32,
    )


def complex_parts(product):
    cols, rows = product.shape[0] // 2, product.shape[1] // 2
    real = product[:cols, :rows] - product[cols:, rows:]
    imag = product[cols:, :rows] + product[:cols, rows:]
    return real, imag


def load_kernel(layer, plan_ref, own_ref, other_ref, _, out_ref, sem):
    layers = own_ref.shape[0]
    own = jnp.max(plan_ref[plan_ref.shape[0] - 1, 0]) == layer // layers
    mine = pltpu.make_async_copy(own_ref.at[layer % layers], out_ref, sem)
    given = pltpu.make_async_copy(other_ref.at[layer % layers], out_ref, sem)
    pl.when(own)(mine.start)
    pl.when(jnp.logical_not(own))(given.start)
    mine.wait()


def image_kernel(layer, kind, first, ready, plan_ref, table_ref, own_ref, other_ref, base_ref, *refs):
    *blocks_refs, out_ref, total_ref, full_ref, weights, sems = refs
    ready_ref = blocks_refs.pop() if ready else None
    wide, rows = total_ref.shape
    cols = wide // 2
    layers, slots = own_ref.shape[:2]
    core = jnp.max(plan_ref[plan_ref.shape[0] - 1, 0])
    used = [jnp.max(plan_ref[layer, slot]) == kind for slot in range(slots)]

    def body(weight_ref):
        copied = [
            pltpu.make_async_copy(weight_ref.at[layer % layers, slot], weights.at[slot], sems.at[slot])
            for slot in range(slots)
        ]
        before = [sum((used[s].astype(jnp.int32) for s in range(slot)), jnp.int32(0)) for slot in range(slots)]
        for slot in range(slots):
            pl.when(used[slot] & (before[slot] < 2))(copied[slot].start)
        base = base_ref[layer] if first else base_ref[...]
        total_ref[...] = base.astype(jnp.float32)
        if len(blocks_refs) == 1:
            assemble(blocks_refs[0], full_ref, 0)
        else:
            for side, blocks_ref in enumerate(blocks_refs):
                pl.when(core == side)(functools.partial(assemble, blocks_ref, full_ref, side))
        for slot in range(slots):

            @pl.when(used[slot])
            def _(slot=slot):
                copied[slot].wait()
                for later in range(slot + 2, slots):
                    pl.when(used[later] & (before[later] == before[slot] + 2))(copied[later].start)
                real, imag = complex_parts(multiply(full_ref[...], weights[slot]))
                cosine = jnp.broadcast_to(table_ref[layer, slot, 0][:, :1], (cols, rows))
                sine = jnp.broadcast_to(table_ref[layer, slot, 1][:, :1], (cols, rows))
                total_ref[:cols] -= real * cosine - imag * sine
                total_ref[cols:] -= real * sine + imag * cosine

    if not ready:
        pl.when(core == layer // layers)(functools.partial(body, own_ref))
    pl.when(core != layer // layers)(functools.partial(body, other_ref))
    if out_ref.ndim == 2:
        out_ref[...] = total_ref[...]
    else:
        total = total_ref[...].astype(jnp.bfloat16)
        if ready:
            total = jnp.where(core == layer // layers, ready_ref[0], total)
        for place in range(out_ref.shape[0]):
            out_ref[place] = total


def inverse_kernel(weight_ref, blocks_ref, *refs):
    parts = sum(ref.ndim == 2 for ref in refs[:-1])
    field_refs, copied_refs, full_ref = refs[:parts], refs[parts:-1], refs[-1]
    assemble(blocks_ref, full_ref, 0)
    real, imag = complex_parts(multiply(full_ref[...], weight_ref[...]))
    real, imag = real.astype(jnp.bfloat16), imag.astype(jnp.bfloat16)
    cols = real.shape[0]
    half = cols // parts
    for part, field_ref in enumerate(field_refs):
        field_ref[:half] = real[part * half : (part + 1) * half]
        field_ref[half:] = imag[part * half : (part + 1) * half]
    for copied_ref in copied_refs:
        for place in range(copied_ref.shape[0]):
            copied_ref[place, :cols] = real
            copied_ref[place, cols:] = imag


def nothing(shapes):
    return list(
        pl.pallas_call(
            lambda *refs: None, out_shape=shapes, out_specs=[ANY] * len(shapes), name="nothing"
        )()
    )


def held(array):
    return pltpu.with_memory_space_constraint(array, pltpu.VMEM)


def far(array):
    return pltpu.with_memory_space_constraint(array, pltpu.HBM)


def local(right_side, inverse, coupling, image_offset, image_count, phase_exponent):
    layers, rows, _, cols = right_side.shape
    slots, unknowns = coupling.shape[1], coupling.shape[4]
    peers = lax.axis_size("angle")
    chips = lax.axis_size("layer") // CORES
    chip, core = jnp.divmod(lax.axis_index("layer"), CORES)
    deep = CORES * layers
    width = cols // CORES
    wide = 2 * width

    def ordered(mine, given):
        return jnp.where(core == 0, jnp.concatenate([mine, given]), jnp.concatenate([given, mine]))

    right = right_side.reshape(layers, rows, 2, CORES, width).transpose(3, 0, 2, 4, 1)
    split = right.reshape(CORES, layers, wide, rows)
    right = ordered(
        jnp.where(core == 0, split[0], split[1]), swap(jnp.where(core == 0, split[1], split[0]))
    )
    kinds = jnp.where(lax.iota(jnp.int32, slots) < image_count[:, None], image_offset, 0)
    both = jnp.stack([kinds, phase_exponent], 1)
    both = ordered(both, swap(both))
    begin = right_side[0].transpose(1, 2, 0).reshape(CORES * wide, rows)
    tied = lax.optimization_barrier((right, both, begin, inverse, coupling))
    right, both, begin, late_inverse, late_coupling = tied
    other_coupling, other_inverse = swap(late_coupling), swap(late_inverse)
    plan = jnp.concatenate([both[:, 0], jnp.full((1, slots), core, jnp.int32)]).astype(jnp.float32)
    plan = jnp.broadcast_to(plan[..., None, None], (deep + 1, slots, 8, 128))
    angle = ((core * width + lax.iota(jnp.int32, width)) // NRHS).astype(jnp.float32)
    phase = (2.0 * math.pi / ANGLES) * both[:, 1].astype(jnp.float32)[:, :, None] * (angle + 0.5)
    table = jnp.stack([jnp.cos(phase), jnp.sin(phase)], 2)
    table = jnp.broadcast_to(table[..., None], table.shape + (128,))

    params = pltpu.CompilerParams(vmem_limit_bytes=LIMIT)
    field_shape = jax.ShapeDtypeStruct((wide, rows), jnp.bfloat16)
    copied_shape = jax.ShapeDtypeStruct((peers, wide, rows), jnp.bfloat16)
    full_scratch = pltpu.VMEM((wide, unknowns), jnp.bfloat16)

    def cost(planes):
        return pl.CostEstimate(
            flops=4 * wide * rows * unknowns * planes,
            bytes_accessed=4 * rows * unknowns * planes,
            transcendentals=0,
        )

    def images(layer, kind, base, blocks, other=None, ready=None):
        blocks = blocks if ready is None else [*blocks, ready]
        return pl.pallas_call(
            functools.partial(image_kernel, layer, kind, base.ndim == 3, ready is not None),
            out_shape=copied_shape if kind == 1 else jax.ShapeDtypeStruct((wide, rows), jnp.float32),
            in_specs=[VMEM] * 2 + [ANY] * 2 + [VMEM] * (1 + len(blocks)),
            out_specs=VMEM,
            scratch_shapes=[
                pltpu.VMEM((wide, rows), jnp.float32),
                full_scratch,
                pltpu.VMEM((slots, 2, rows, unknowns), jnp.bfloat16),
                pltpu.SemaphoreType.DMA((slots,)),
            ],
            compiler_params=params,
            cost_estimate=cost(slots // 2),
            name="images_%d" % kind,
        )(plan, table, far(coupling), far(other_coupling if other is None else other), base, *blocks)

    def invert(blocks, weights, last):
        parts = blocks.shape[1] // wide
        out_shape = [field_shape] * parts + [jax.ShapeDtypeStruct(blocks.shape, jnp.bfloat16)] * (not last)
        return pl.pallas_call(
            inverse_kernel,
            out_shape=out_shape,
            in_specs=[VMEM] * 2,
            out_specs=[VMEM] * len(out_shape),
            scratch_shapes=[pltpu.VMEM((parts * wide, unknowns), jnp.bfloat16)],
            compiler_params=params,
            cost_estimate=cost(1),
            name="invert",
        )(held(weights), blocks)

    def load(layer, other, after):
        return pl.pallas_call(
            functools.partial(load_kernel, layer),
            out_shape=pltpu.VMEM(inverse.shape[1:], inverse.dtype),
            in_specs=[VMEM] + [ANY] * 3,
            out_specs=VMEM,
            scratch_shapes=[pltpu.SemaphoreType.DMA],
            compiler_params=pltpu.CompilerParams(vmem_limit_bytes=2**20),
            cost_estimate=pl.CostEstimate(flops=0, bytes_accessed=inverse.size * 2, transcendentals=0),
            name="load",
        )(plan, far(inverse), far(other), after)

    def run(start, latest, earlier, ready=None):
        fields = []
        for layer in range(start, deep):
            base = right if earlier is None else images(layer, 2, right, earlier)
            copied = images(layer, 1, base, latest, ready=ready if layer == start else None)
            if layer + 1 < deep:
                field, next_copied = invert(gather(copied), load(layer, other_inverse, copied), False)
                fields.append(field)
                earlier, latest = latest, [gather(next_copied)]
        return [*fields, copied, *latest]

    def finish(copied):
        return list(invert(gather(copied), load(deep - 1, other_inverse, copied), True))

    def only(here, shapes, function, *operands):
        return lax.cond(here, function, lambda *_: nothing(shapes), *operands)

    found = []
    field = earlier = None
    for number in range(chips):
        if number == 0:
            gathered = jax.ShapeDtypeStruct((peers, CORES * wide, rows), jnp.bfloat16)

            def layer_zero(begin):
                copied = copies(begin, peers)
                *fields, copied = invert(gather(copied), load(0, inverse, copied), False)
                latest = gather(copied)
                return [*fields, latest, images(1, 1, right, [latest], other=coupling)]

            shapes = [field_shape] * CORES + [gathered, copied_shape]
            *zero, latest, ready = only((chip == 0) & (core == 0), shapes, layer_zero, begin)
            pairs = [(b, peers + b) for b in range(peers)]
            given = lax.ppermute(latest, ("layer", "angle"), pairs)
            start, function, operands = 1, lambda ready, *latest: run(1, latest, None, ready), (ready, latest, given)
        else:

            def function(field, earlier):
                return run(0, [gather(copies(field, peers))], [earlier])

            start, operands = 0, (field, earlier)
        here = chip == number
        shapes = [field_shape] * (deep - start - 1) + [copied_shape] * 2
        *fields, copied, latest = only(here, shapes, function, *operands)
        if number + 1 < chips:
            earlier = shift(latest, number)
        (last,) = only(here, [field_shape], finish, copied)
        found.append((zero[:1] if start else []) + fields + [last])
        if number + 1 < chips:
            field = shift(last, number)

    chosen = []
    for layer in range(deep):
        value = found[0][layer]
        for number in range(1, chips):
            value = jnp.where(chip == number, found[number][layer], value)
        chosen.append(value)
    low, high = jnp.stack(chosen[:layers]), jnp.stack(chosen[layers:])
    mine = jnp.where(core == 0, low, high)
    given = swap(jnp.where(core == 0, high, low))
    first_given = jnp.where(chip == 0, jnp.where(core == 0, zero[1], given[0]), given[0])
    given = jnp.concatenate([first_given[None], given[1:]])
    result = jnp.where(core == 0, jnp.stack([mine, given]), jnp.stack([given, mine]))
    result = result.reshape(CORES, layers, 2, width, rows).transpose(1, 4, 2, 0, 3)
    return result.reshape(layers, rows, 2, cols)


def solution(mesh):
    placed = (
        P("layer", "angle", None, None),
        P("layer", None, "angle", None),
        P("layer", None, None, "angle", None),
        P("layer", None),
        P("layer"),
        P("layer", None),
    )
    return jax.shard_map(
        local,
        mesh=mesh,
        in_specs=placed,
        out_specs=P("layer", "angle", None, None),
        check_vma=False,
    )
```

```python
import functools
import math

import jax
import jax.numpy as jnp
from jax import lax
from jax.experimental import pallas as pl
from jax.experimental.pallas import tpu as pltpu
from jax.sharding import PartitionSpec as P

ANGLES = 16
NRHS = 6
CORES = 2
LIMIT = 24 * 2**20

VMEM = pl.BlockSpec(memory_space=pltpu.VMEM)
ANY = pl.BlockSpec(memory_space=pl.ANY)


def copies_kernel(source_ref, out_ref):
    for place in range(out_ref.shape[0]):
        out_ref[place] = source_ref[...]


def copies(array, count):
    return pl.pallas_call(
        copies_kernel,
        out_shape=jax.ShapeDtypeStruct((count,) + array.shape, array.dtype),
        in_specs=[VMEM],
        out_specs=VMEM,
        compiler_params=pltpu.CompilerParams(vmem_limit_bytes=LIMIT),
        name="copies",
    )(array)


def swap(array):
    pairs = [(i, i ^ 1) for i in range(lax.axis_size("layer"))]
    return lax.ppermute(array, "layer", pairs)


def shift(array, chip):
    peers = lax.axis_size("angle")
    first, last = chip * CORES * peers, (chip + 1) * CORES * peers
    return lax.ppermute(array, ("layer", "angle"), [(i, i + CORES * peers) for i in range(first, last)])


def gather(copied):
    return lax.all_to_all(copied, "angle", 0, 0)


def assemble(blocks_ref, full_ref, side):
    lines, width = full_ref.shape[0], blocks_ref.shape[2]
    half, whole = lines // 2, blocks_ref.shape[1] // 2
    for owner in range(blocks_ref.shape[0]):
        columns = slice(owner * width, (owner + 1) * width)
        for part in range(2):
            first = part * whole + side * half
            full_ref[part * half : (part + 1) * half, columns] = blocks_ref[owner, first : first + half]


def multiply(full, weights):
    return lax.dot_general(
        full,
        weights.reshape(-1, weights.shape[2]),
        (((1,), (1,)), ((), ())),
        preferred_element_type=jnp.float32,
    )


def complex_parts(product):
    cols, rows = product.shape[0] // 2, product.shape[1] // 2
    real = product[:cols, :rows] - product[cols:, rows:]
    imag = product[cols:, :rows] + product[:cols, rows:]
    return real, imag


def load_kernel(layer, plan_ref, own_ref, other_ref, _, out_ref, sem):
    layers = own_ref.shape[0]
    own = jnp.max(plan_ref[plan_ref.shape[0] - 1, 0]) == layer // layers
    mine = pltpu.make_async_copy(own_ref.at[layer % layers], out_ref, sem)
    given = pltpu.make_async_copy(other_ref.at[layer % layers], out_ref, sem)
    pl.when(own)(mine.start)
    pl.when(jnp.logical_not(own))(given.start)
    mine.wait()


def image_kernel(layer, kind, first, plan_ref, table_ref, own_ref, other_ref, base_ref, *refs):
    *blocks_refs, out_ref, total_ref, full_ref, weights, sems = refs
    wide, rows = total_ref.shape
    cols = wide // 2
    layers, slots = own_ref.shape[:2]
    core = jnp.max(plan_ref[plan_ref.shape[0] - 1, 0])
    used = [jnp.max(plan_ref[layer, slot]) == kind for slot in range(slots)]

    def body(weight_ref):
        copied = [
            pltpu.make_async_copy(weight_ref.at[layer % layers, slot], weights.at[slot], sems.at[slot])
            for slot in range(slots)
        ]
        before = [sum((used[s].astype(jnp.int32) for s in range(slot)), jnp.int32(0)) for slot in range(slots)]
        for slot in range(slots):
            pl.when(used[slot] & (before[slot] < 2))(copied[slot].start)
        base = base_ref[layer] if first else base_ref[...]
        total_ref[...] = base.astype(jnp.float32)
        if len(blocks_refs) == 1:
            assemble(blocks_refs[0], full_ref, 0)
        else:
            for side, blocks_ref in enumerate(blocks_refs):
                pl.when(core == side)(functools.partial(assemble, blocks_ref, full_ref, side))
        for slot in range(slots):

            @pl.when(used[slot])
            def _(slot=slot):
                copied[slot].wait()
                for later in range(slot + 2, slots):
                    pl.when(used[later] & (before[later] == before[slot] + 2))(copied[later].start)
                real, imag = complex_parts(multiply(full_ref[...], weights[slot]))
                cosine = jnp.broadcast_to(table_ref[layer, slot, 0][:, :1], (cols, rows))
                sine = jnp.broadcast_to(table_ref[layer, slot, 1][:, :1], (cols, rows))
                total_ref[:cols] -= real * cosine - imag * sine
                total_ref[cols:] -= real * sine + imag * cosine

    pl.when(core == layer // layers)(functools.partial(body, own_ref))
    pl.when(core != layer // layers)(functools.partial(body, other_ref))
    if out_ref.ndim == 2:
        out_ref[...] = total_ref[...]
    else:
        total = total_ref[...].astype(jnp.bfloat16)
        for place in range(out_ref.shape[0]):
            out_ref[place] = total


def inverse_kernel(weight_ref, blocks_ref, *refs):
    parts = sum(ref.ndim == 2 for ref in refs[:-1])
    field_refs, copied_refs, full_ref = refs[:parts], refs[parts:-1], refs[-1]
    assemble(blocks_ref, full_ref, 0)
    real, imag = complex_parts(multiply(full_ref[...], weight_ref[...]))
    real, imag = real.astype(jnp.bfloat16), imag.astype(jnp.bfloat16)
    cols = real.shape[0]
    half = cols // parts
    for part, field_ref in enumerate(field_refs):
        field_ref[:half] = real[part * half : (part + 1) * half]
        field_ref[half:] = imag[part * half : (part + 1) * half]
    for copied_ref in copied_refs:
        for place in range(copied_ref.shape[0]):
            copied_ref[place, :cols] = real
            copied_ref[place, cols:] = imag


def nothing(shapes):
    return list(
        pl.pallas_call(
            lambda *refs: None, out_shape=shapes, out_specs=[ANY] * len(shapes), name="nothing"
        )()
    )


def held(array):
    return pltpu.with_memory_space_constraint(array, pltpu.VMEM)


def far(array):
    return pltpu.with_memory_space_constraint(array, pltpu.HBM)


def local(right_side, inverse, coupling, image_offset, image_count, phase_exponent):
    layers, rows, _, cols = right_side.shape
    slots, unknowns = coupling.shape[1], coupling.shape[4]
    peers = lax.axis_size("angle")
    chips = lax.axis_size("layer") // CORES
    chip, core = jnp.divmod(lax.axis_index("layer"), CORES)
    deep = CORES * layers
    width = cols // CORES
    wide = 2 * width

    def ordered(mine, given):
        return jnp.where(core == 0, jnp.concatenate([mine, given]), jnp.concatenate([given, mine]))

    right = right_side.reshape(layers, rows, 2, CORES, width).transpose(3, 0, 2, 4, 1)
    split = right.reshape(CORES, layers, wide, rows)
    right = ordered(
        jnp.where(core == 0, split[0], split[1]), swap(jnp.where(core == 0, split[1], split[0]))
    )
    kinds = jnp.where(lax.iota(jnp.int32, slots) < image_count[:, None], image_offset, 0)
    both = jnp.stack([kinds, phase_exponent], 1)
    both = ordered(both, swap(both))
    begin = right_side[0].transpose(1, 2, 0).reshape(CORES * wide, rows)
    tied = lax.optimization_barrier((right, both, begin, inverse, coupling))
    right, both, begin, late_inverse, late_coupling = tied
    other_coupling, other_inverse = swap(late_coupling), swap(late_inverse)
    plan = jnp.concatenate([both[:, 0], jnp.full((1, slots), core, jnp.int32)]).astype(jnp.float32)
    plan = jnp.broadcast_to(plan[..., None, None], (deep + 1, slots, 8, 128))
    angle = ((core * width + lax.iota(jnp.int32, width)) // NRHS).astype(jnp.float32)
    phase = (2.0 * math.pi / ANGLES) * both[:, 1].astype(jnp.float32)[:, :, None] * (angle + 0.5)
    table = jnp.stack([jnp.cos(phase), jnp.sin(phase)], 2)
    table = jnp.broadcast_to(table[..., None], table.shape + (128,))

    params = pltpu.CompilerParams(vmem_limit_bytes=LIMIT)
    field_shape = jax.ShapeDtypeStruct((wide, rows), jnp.bfloat16)
    copied_shape = jax.ShapeDtypeStruct((peers, wide, rows), jnp.bfloat16)
    full_scratch = pltpu.VMEM((wide, unknowns), jnp.bfloat16)

    def cost(planes):
        return pl.CostEstimate(
            flops=4 * wide * rows * unknowns * planes,
            bytes_accessed=4 * rows * unknowns * planes,
            transcendentals=0,
        )

    def images(layer, kind, base, blocks):
        return pl.pallas_call(
            functools.partial(image_kernel, layer, kind, base.ndim == 3),
            out_shape=copied_shape if kind == 1 else jax.ShapeDtypeStruct((wide, rows), jnp.float32),
            in_specs=[VMEM] * 2 + [ANY] * 2 + [VMEM] * (1 + len(blocks)),
            out_specs=VMEM,
            scratch_shapes=[
                pltpu.VMEM((wide, rows), jnp.float32),
                full_scratch,
                pltpu.VMEM((slots, 2, rows, unknowns), jnp.bfloat16),
                pltpu.SemaphoreType.DMA((slots,)),
            ],
            compiler_params=params,
            cost_estimate=cost(slots // 2),
            name="images_%d" % kind,
        )(plan, table, far(coupling), far(other_coupling), base, *blocks)

    def invert(blocks, weights, last):
        parts = blocks.shape[1] // wide
        out_shape = [field_shape] * parts + [jax.ShapeDtypeStruct(blocks.shape, jnp.bfloat16)] * (not last)
        return pl.pallas_call(
            inverse_kernel,
            out_shape=out_shape,
            in_specs=[VMEM] * 2,
            out_specs=[VMEM] * len(out_shape),
            scratch_shapes=[pltpu.VMEM((parts * wide, unknowns), jnp.bfloat16)],
            compiler_params=params,
            cost_estimate=cost(1),
            name="invert",
        )(held(weights), blocks)

    def load(layer, other, after):
        return pl.pallas_call(
            functools.partial(load_kernel, layer),
            out_shape=pltpu.VMEM(inverse.shape[1:], inverse.dtype),
            in_specs=[VMEM] + [ANY] * 3,
            out_specs=VMEM,
            scratch_shapes=[pltpu.SemaphoreType.DMA],
            compiler_params=pltpu.CompilerParams(vmem_limit_bytes=2**20),
            cost_estimate=pl.CostEstimate(flops=0, bytes_accessed=inverse.size * 2, transcendentals=0),
            name="load",
        )(plan, far(inverse), far(other), after)

    def run(start, latest, earlier):
        fields = []
        for layer in range(start, deep):
            base = right if earlier is None else images(layer, 2, right, earlier)
            copied = images(layer, 1, base, latest)
            if layer + 1 < deep:
                field, next_copied = invert(gather(copied), load(layer, other_inverse, copied), False)
                fields.append(field)
                earlier, latest = latest, [gather(next_copied)]
        return [*fields, copied, *latest]

    def finish(copied):
        return list(invert(gather(copied), load(deep - 1, other_inverse, copied), True))

    def only(here, shapes, function, *operands):
        return lax.cond(here, function, lambda *_: nothing(shapes), *operands)

    found = []
    field = earlier = None
    for number in range(chips):
        if number == 0:
            gathered = jax.ShapeDtypeStruct((peers, CORES * wide, rows), jnp.bfloat16)

            def layer_zero(begin):
                copied = copies(begin, peers)
                *fields, copied = invert(gather(copied), load(0, inverse, copied), False)
                return [*fields, gather(copied)]

            begin, _ = lax.optimization_barrier((begin, table))
            shapes = [field_shape] * CORES + [gathered]
            *zero, latest = only((chip == 0) & (core == 0), shapes, layer_zero, begin)
            pairs = [(b, peers + b) for b in range(peers)]
            given = lax.ppermute(latest, ("layer", "angle"), pairs)
            start, function, operands = 1, lambda *latest: run(1, latest, None), (latest, given)
        else:

            def function(field, earlier):
                return run(0, [gather(copies(field, peers))], [earlier])

            start, operands = 0, (field, earlier)
        here = chip == number
        shapes = [field_shape] * (deep - start - 1) + [copied_shape] * 2
        *fields, copied, latest = only(here, shapes, function, *operands)
        if number + 1 < chips:
            earlier = shift(latest, number)
        (last,) = only(here, [field_shape], finish, copied)
        found.append((zero[:1] if start else []) + fields + [last])
        if number + 1 < chips:
            field = shift(last, number)

    chosen = []
    for layer in range(deep):
        value = found[0][layer]
        for number in range(1, chips):
            value = jnp.where(chip == number, found[number][layer], value)
        chosen.append(value)
    low, high = jnp.stack(chosen[:layers]), jnp.stack(chosen[layers:])
    mine = jnp.where(core == 0, low, high)
    given = swap(jnp.where(core == 0, high, low))
    first_given = jnp.where(chip == 0, jnp.where(core == 0, zero[1], given[0]), given[0])
    given = jnp.concatenate([first_given[None], given[1:]])
    result = jnp.where(core == 0, jnp.stack([mine, given]), jnp.stack([given, mine]))
    result = result.reshape(CORES, layers, 2, width, rows).transpose(1, 4, 2, 0, 3)
    return result.reshape(layers, rows, 2, cols)


def solution(mesh):
    placed = (
        P("layer", "angle", None, None),
        P("layer", None, "angle", None),
        P("layer", None, None, "angle", None),
        P("layer", None),
        P("layer"),
        P("layer", None),
    )
    return jax.shard_map(
        local,
        mesh=mesh,
        in_specs=placed,
        out_specs=P("layer", "angle", None, None),
        check_vma=False,
    )
```

```python
import functools
import math

import jax
import jax.numpy as jnp
from jax import lax
from jax.experimental import pallas as pl
from jax.experimental.pallas import tpu as pltpu
from jax.sharding import PartitionSpec as P

ANGLES = 16
NRHS = 6
CORES = 2
LIMIT = 24 * 2**20

VMEM = pl.BlockSpec(memory_space=pltpu.VMEM)
ANY = pl.BlockSpec(memory_space=pl.ANY)


def copies_kernel(source_ref, out_ref):
    for place in range(out_ref.shape[0]):
        out_ref[place] = source_ref[...]


def copies(array, count):
    return pl.pallas_call(
        copies_kernel,
        out_shape=jax.ShapeDtypeStruct((count,) + array.shape, array.dtype),
        in_specs=[VMEM],
        out_specs=VMEM,
        compiler_params=pltpu.CompilerParams(vmem_limit_bytes=LIMIT),
        name="copies",
    )(array)


def swap(array):
    pairs = [(i, i ^ 1) for i in range(lax.axis_size("layer"))]
    return lax.ppermute(array, "layer", pairs)


def shift(array, chip):
    peers = lax.axis_size("angle")
    first, last = chip * CORES * peers, (chip + 1) * CORES * peers
    return lax.ppermute(array, ("layer", "angle"), [(i, i + CORES * peers) for i in range(first, last)])


def gather(copied):
    return lax.all_to_all(copied, "angle", 0, 0)


def assemble(blocks_ref, full_ref, side):
    lines, width = full_ref.shape[0], blocks_ref.shape[2]
    half, whole = lines // 2, blocks_ref.shape[1] // 2
    for owner in range(blocks_ref.shape[0]):
        columns = slice(owner * width, (owner + 1) * width)
        for part in range(2):
            first = part * whole + side * half
            full_ref[part * half : (part + 1) * half, columns] = blocks_ref[owner, first : first + half]


def multiply(full, weights):
    return lax.dot_general(
        full,
        weights.reshape(-1, weights.shape[2]),
        (((1,), (1,)), ((), ())),
        preferred_element_type=jnp.float32,
    )


def complex_parts(product):
    cols, rows = product.shape[0] // 2, product.shape[1] // 2
    real = product[:cols, :rows] - product[cols:, rows:]
    imag = product[cols:, :rows] + product[:cols, rows:]
    return real, imag


def load_kernel(layer, plan_ref, own_ref, other_ref, _, out_ref, sem):
    layers = own_ref.shape[0]
    own = jnp.max(plan_ref[plan_ref.shape[0] - 1, 0]) == layer // layers
    mine = pltpu.make_async_copy(own_ref.at[layer % layers], out_ref, sem)
    given = pltpu.make_async_copy(other_ref.at[layer % layers], out_ref, sem)
    pl.when(own)(mine.start)
    pl.when(jnp.logical_not(own))(given.start)
    mine.wait()


def image_kernel(layer, kind, first, plan_ref, table_ref, own_ref, other_ref, base_ref, *refs):
    *blocks_refs, out_ref, total_ref, full_ref, weights, sems = refs
    wide, rows = total_ref.shape
    cols = wide // 2
    layers, slots = own_ref.shape[:2]
    core = jnp.max(plan_ref[plan_ref.shape[0] - 1, 0])
    own = core == layer // layers

    def copy(weight_ref, slot):
        return pltpu.make_async_copy(weight_ref.at[layer % layers, slot], weights.at[slot], sems.at[slot])

    for slot in range(slots):
        used = jnp.max(plan_ref[layer, slot]) == kind
        pl.when(used & own)(copy(own_ref, slot).start)
        pl.when(used & jnp.logical_not(own))(copy(other_ref, slot).start)
    base = base_ref[layer] if first else base_ref[...]
    total_ref[...] = base.astype(jnp.float32)
    if len(blocks_refs) == 1:
        assemble(blocks_refs[0], full_ref, 0)
    else:
        for side, blocks_ref in enumerate(blocks_refs):
            pl.when(core == side)(functools.partial(assemble, blocks_ref, full_ref, side))

    def subtract(slot, _):
        @pl.when(jnp.max(plan_ref[layer, slot]) == kind)
        def _():
            copy(own_ref, slot).wait()
            real, imag = complex_parts(multiply(full_ref[...], weights[slot]))
            cosine = jnp.broadcast_to(table_ref[layer, slot, 0][:, :1], (cols, rows))
            sine = jnp.broadcast_to(table_ref[layer, slot, 1][:, :1], (cols, rows))
            total_ref[:cols] -= real * cosine - imag * sine
            total_ref[cols:] -= real * sine + imag * cosine

        return 0

    lax.fori_loop(0, slots, subtract, 0)
    if out_ref.ndim == 2:
        out_ref[...] = total_ref[...]
    else:
        total = total_ref[...].astype(jnp.bfloat16)
        for place in range(out_ref.shape[0]):
            out_ref[place] = total


def inverse_kernel(weight_ref, blocks_ref, *refs):
    parts = sum(ref.ndim == 2 for ref in refs[:-1])
    field_refs, copied_refs, full_ref = refs[:parts], refs[parts:-1], refs[-1]
    assemble(blocks_ref, full_ref, 0)
    real, imag = complex_parts(multiply(full_ref[...], weight_ref[...]))
    real, imag = real.astype(jnp.bfloat16), imag.astype(jnp.bfloat16)
    cols = real.shape[0]
    half = cols // parts
    for part, field_ref in enumerate(field_refs):
        field_ref[:half] = real[part * half : (part + 1) * half]
        field_ref[half:] = imag[part * half : (part + 1) * half]
    for copied_ref in copied_refs:
        for place in range(copied_ref.shape[0]):
            copied_ref[place, :cols] = real
            copied_ref[place, cols:] = imag


def nothing(shapes):
    return list(
        pl.pallas_call(
            lambda *refs: None, out_shape=shapes, out_specs=[ANY] * len(shapes), name="nothing"
        )()
    )


def held(array):
    return pltpu.with_memory_space_constraint(array, pltpu.VMEM)


def far(array):
    return pltpu.with_memory_space_constraint(array, pltpu.HBM)


def local(right_side, inverse, coupling, image_offset, image_count, phase_exponent):
    layers, rows, _, cols = right_side.shape
    slots, unknowns = coupling.shape[1], coupling.shape[4]
    peers = lax.axis_size("angle")
    chips = lax.axis_size("layer") // CORES
    chip, core = jnp.divmod(lax.axis_index("layer"), CORES)
    deep = CORES * layers
    width = cols // CORES
    wide = 2 * width

    def ordered(mine, given):
        return jnp.where(core == 0, jnp.concatenate([mine, given]), jnp.concatenate([given, mine]))

    right = right_side.reshape(layers, rows, 2, CORES, width).transpose(3, 0, 2, 4, 1)
    split = right.reshape(CORES, layers, wide, rows)
    right = ordered(
        jnp.where(core == 0, split[0], split[1]), swap(jnp.where(core == 0, split[1], split[0]))
    )
    kinds = jnp.where(lax.iota(jnp.int32, slots) < image_count[:, None], image_offset, 0)
    both = jnp.stack([kinds, phase_exponent], 1)
    both = ordered(both, swap(both))
    begin = right_side[0].transpose(1, 2, 0).reshape(CORES * wide, rows)
    tied = lax.optimization_barrier((right, both, begin, inverse, coupling))
    right, both, begin, late_inverse, late_coupling = tied
    other_coupling, other_inverse = swap(late_coupling), swap(late_inverse)
    plan = jnp.concatenate([both[:, 0], jnp.full((1, slots), core, jnp.int32)]).astype(jnp.float32)
    plan = jnp.broadcast_to(plan[..., None, None], (deep + 1, slots, 8, 128))
    angle = ((core * width + lax.iota(jnp.int32, width)) // NRHS).astype(jnp.float32)
    phase = (2.0 * math.pi / ANGLES) * both[:, 1].astype(jnp.float32)[:, :, None] * (angle + 0.5)
    table = jnp.stack([jnp.cos(phase), jnp.sin(phase)], 2)
    table = jnp.broadcast_to(table[..., None], table.shape + (128,))

    params = pltpu.CompilerParams(vmem_limit_bytes=LIMIT)
    field_shape = jax.ShapeDtypeStruct((wide, rows), jnp.bfloat16)
    copied_shape = jax.ShapeDtypeStruct((peers, wide, rows), jnp.bfloat16)
    full_scratch = pltpu.VMEM((wide, unknowns), jnp.bfloat16)

    def cost(planes):
        return pl.CostEstimate(
            flops=4 * wide * rows * unknowns * planes,
            bytes_accessed=4 * rows * unknowns * planes,
            transcendentals=0,
        )

    def images(layer, kind, base, blocks):
        return pl.pallas_call(
            functools.partial(image_kernel, layer, kind, base.ndim == 3),
            out_shape=copied_shape if kind == 1 else jax.ShapeDtypeStruct((wide, rows), jnp.float32),
            in_specs=[VMEM] * 2 + [ANY] * 2 + [VMEM] * (1 + len(blocks)),
            out_specs=VMEM,
            scratch_shapes=[
                pltpu.VMEM((wide, rows), jnp.float32),
                full_scratch,
                pltpu.VMEM((slots, 2, rows, unknowns), jnp.bfloat16),
                pltpu.SemaphoreType.DMA((slots,)),
            ],
            compiler_params=params,
            cost_estimate=cost(slots // 2),
            name="images_%d" % kind,
        )(plan, table, far(coupling), far(other_coupling), base, *blocks)

    def invert(blocks, weights, last):
        parts = blocks.shape[1] // wide
        out_shape = [field_shape] * parts + [jax.ShapeDtypeStruct(blocks.shape, jnp.bfloat16)] * (not last)
        return pl.pallas_call(
            inverse_kernel,
            out_shape=out_shape,
            in_specs=[VMEM] * 2,
            out_specs=[VMEM] * len(out_shape),
            scratch_shapes=[pltpu.VMEM((parts * wide, unknowns), jnp.bfloat16)],
            compiler_params=params,
            cost_estimate=cost(1),
            name="invert",
        )(held(weights), blocks)

    def load(layer, other, after):
        return pl.pallas_call(
            functools.partial(load_kernel, layer),
            out_shape=pltpu.VMEM(inverse.shape[1:], inverse.dtype),
            in_specs=[VMEM] + [ANY] * 3,
            out_specs=VMEM,
            scratch_shapes=[pltpu.SemaphoreType.DMA],
            compiler_params=pltpu.CompilerParams(vmem_limit_bytes=2**20),
            cost_estimate=pl.CostEstimate(flops=0, bytes_accessed=inverse.size * 2, transcendentals=0),
            name="load",
        )(plan, far(inverse), far(other), after)

    def run(start, latest, earlier):
        fields = []
        for layer in range(start, deep):
            base = right if earlier is None else images(layer, 2, right, earlier)
            copied = images(layer, 1, base, latest)
            if layer + 1 < deep:
                field, next_copied = invert(gather(copied), load(layer, other_inverse, copied), False)
                fields.append(field)
                earlier, latest = latest, [gather(next_copied)]
        return [*fields, copied, *latest]

    def finish(copied):
        return list(invert(gather(copied), load(deep - 1, other_inverse, copied), True))

    def only(here, shapes, function, *operands):
        return lax.cond(here, function, lambda *_: nothing(shapes), *operands)

    found = []
    field = earlier = None
    for number in range(chips):
        if number == 0:
            gathered = jax.ShapeDtypeStruct((peers, CORES * wide, rows), jnp.bfloat16)

            def layer_zero(begin):
                copied = copies(begin, peers)
                *fields, copied = invert(gather(copied), load(0, inverse, copied), False)
                return [*fields, gather(copied)]

            begin, _ = lax.optimization_barrier((begin, table))
            shapes = [field_shape] * CORES + [gathered]
            *zero, latest = only((chip == 0) & (core == 0), shapes, layer_zero, begin)
            pairs = [(b, peers + b) for b in range(peers)]
            given = lax.ppermute(latest, ("layer", "angle"), pairs)
            start, function, operands = 1, lambda *latest: run(1, latest, None), (latest, given)
        else:

            def function(field, earlier):
                return run(0, [gather(copies(field, peers))], [earlier])

            start, operands = 0, (field, earlier)
        here = chip == number
        shapes = [field_shape] * (deep - start - 1) + [copied_shape] * 2
        *fields, copied, latest = only(here, shapes, function, *operands)
        if number + 1 < chips:
            earlier = shift(latest, number)
        (last,) = only(here, [field_shape], finish, copied)
        found.append((zero[:1] if start else []) + fields + [last])
        if number + 1 < chips:
            field = shift(last, number)

    chosen = []
    for layer in range(deep):
        value = found[0][layer]
        for number in range(1, chips):
            value = jnp.where(chip == number, found[number][layer], value)
        chosen.append(value)
    low, high = jnp.stack(chosen[:layers]), jnp.stack(chosen[layers:])
    mine = jnp.where(core == 0, low, high)
    given = swap(jnp.where(core == 0, high, low))
    first_given = jnp.where(chip == 0, jnp.where(core == 0, zero[1], given[0]), given[0])
    given = jnp.concatenate([first_given[None], given[1:]])
    result = jnp.where(core == 0, jnp.stack([mine, given]), jnp.stack([given, mine]))
    result = result.reshape(CORES, layers, 2, width, rows).transpose(1, 4, 2, 0, 3)
    return result.reshape(layers, rows, 2, cols)


def solution(mesh):
    placed = (
        P("layer", "angle", None, None),
        P("layer", None, "angle", None),
        P("layer", None, None, "angle", None),
        P("layer", None),
        P("layer"),
        P("layer", None),
    )
    return jax.shard_map(
        local,
        mesh=mesh,
        in_specs=placed,
        out_specs=P("layer", "angle", None, None),
        check_vma=False,
    )
```

```python
import functools
import math

import jax
import jax.numpy as jnp
from jax import lax
from jax.experimental import pallas as pl
from jax.experimental.pallas import tpu as pltpu
from jax.sharding import PartitionSpec as P

ANGLES = 16
NRHS = 6
CORES = 2
LIMIT = 24 * 2**20

VMEM = pl.BlockSpec(memory_space=pltpu.VMEM)
ANY = pl.BlockSpec(memory_space=pl.ANY)


def copies_kernel(source_ref, out_ref):
    for place in range(out_ref.shape[0]):
        out_ref[place] = source_ref[...]


def copies(array, count):
    return pl.pallas_call(
        copies_kernel,
        out_shape=jax.ShapeDtypeStruct((count,) + array.shape, array.dtype),
        in_specs=[VMEM],
        out_specs=VMEM,
        compiler_params=pltpu.CompilerParams(vmem_limit_bytes=LIMIT),
        name="copies",
    )(array)


def swap(array):
    pairs = [(i, i ^ 1) for i in range(lax.axis_size("layer"))]
    return lax.ppermute(array, "layer", pairs)


def shift(array, chip):
    peers = lax.axis_size("angle")
    first, last = chip * CORES * peers, (chip + 1) * CORES * peers
    return lax.ppermute(array, ("layer", "angle"), [(i, i + CORES * peers) for i in range(first, last)])


def gather(copied):
    return lax.all_to_all(copied, "angle", 0, 0)


def assemble(blocks_ref, full_ref, side):
    lines, width = full_ref.shape[0], blocks_ref.shape[2]
    half, whole = lines // 2, blocks_ref.shape[1] // 2
    for owner in range(blocks_ref.shape[0]):
        columns = slice(owner * width, (owner + 1) * width)
        for part in range(2):
            first = part * whole + side * half
            full_ref[part * half : (part + 1) * half, columns] = blocks_ref[owner, first : first + half]


def multiply(full, weights):
    return lax.dot_general(
        full,
        weights.reshape(-1, weights.shape[2]),
        (((1,), (1,)), ((), ())),
        preferred_element_type=jnp.float32,
    )


def complex_parts(product):
    cols, rows = product.shape[0] // 2, product.shape[1] // 2
    real = product[:cols, :rows] - product[cols:, rows:]
    imag = product[cols:, :rows] + product[:cols, rows:]
    return real, imag


def load_kernel(layer, plan_ref, own_ref, other_ref, _, out_ref, sem):
    layers = own_ref.shape[0]
    own = jnp.max(plan_ref[plan_ref.shape[0] - 1, 0]) == layer // layers
    mine = pltpu.make_async_copy(own_ref.at[layer % layers], out_ref, sem)
    given = pltpu.make_async_copy(other_ref.at[layer % layers], out_ref, sem)
    pl.when(own)(mine.start)
    pl.when(jnp.logical_not(own))(given.start)
    mine.wait()


def image_kernel(layer, kind, first, ahead, plan_ref, table_ref, own_ref, other_ref, base_ref, *refs):
    *blocks_refs, out_ref, total_ref, full_ref, weights, sems = refs
    ahead_ref = None
    if ahead and kind == 1:
        ahead_ref = blocks_refs.pop()
    elif ahead:
        out_ref, ahead_ref = blocks_refs.pop(), out_ref
    wide, rows = total_ref.shape
    cols = wide // 2
    layers, slots = own_ref.shape[:2]
    core = jnp.max(plan_ref[plan_ref.shape[0] - 1, 0])
    own = core == layer // layers

    def copy(weight_ref, slot):
        return pltpu.make_async_copy(weight_ref.at[layer % layers, slot], weights.at[slot], sems.at[slot])

    found = jnp.int32(0)
    for slot in range(slots):
        used = jnp.max(plan_ref[layer, slot]) == kind
        wanted = used & (found > 0) if ahead and kind == 1 else used
        pl.when(wanted & own)(copy(own_ref, slot).start)
        pl.when(wanted & jnp.logical_not(own))(copy(other_ref, slot).start)
        found = found + used.astype(jnp.int32)
    if ahead and kind == 2:
        next_found = jnp.int32(0)
        for slot in range(slots):
            used = jnp.max(plan_ref[layer, slot]) == 1
            wanted = used & (next_found == 0)
            for mine, weight_ref in ((own, own_ref), (jnp.logical_not(own), other_ref)):
                source = weight_ref.at[layer % layers, slot]
                fetch = pltpu.make_async_copy(source, ahead_ref, sems.at[slots])
                pl.when(wanted & mine)(fetch.start)
            next_found = next_found + used.astype(jnp.int32)
    base = base_ref[layer] if first else base_ref[...]
    total_ref[...] = base.astype(jnp.float32)
    if len(blocks_refs) == 1:
        assemble(blocks_refs[0], full_ref, 0)
    else:
        for side, blocks_ref in enumerate(blocks_refs):
            pl.when(core == side)(functools.partial(assemble, blocks_ref, full_ref, side))

    def subtract(slot, weight):
        real, imag = complex_parts(multiply(full_ref[...], weight))
        cosine = jnp.broadcast_to(table_ref[layer, slot, 0][:, :1], (cols, rows))
        sine = jnp.broadcast_to(table_ref[layer, slot, 1][:, :1], (cols, rows))
        total_ref[:cols] -= real * cosine - imag * sine
        total_ref[cols:] -= real * sine + imag * cosine

    def step(slot, done):
        used = jnp.max(plan_ref[layer, slot]) == kind
        there = used & (done == 0) if ahead and kind == 1 else used & False

        @pl.when(used & jnp.logical_not(there))
        def _():
            copy(own_ref, slot).wait()
            subtract(slot, weights[slot])

        if ahead and kind == 1:
            pl.when(there)(lambda: subtract(slot, ahead_ref[...]))
        return done + used.astype(jnp.int32)

    lax.fori_loop(0, slots, step, jnp.int32(0))
    if ahead and kind == 2:

        @pl.when(next_found > 0)
        def _():
            pltpu.make_async_copy(own_ref.at[layer % layers, 0], ahead_ref, sems.at[slots]).wait()

    if out_ref.ndim == 2:
        out_ref[...] = total_ref[...]
    else:
        total = total_ref[...].astype(jnp.bfloat16)
        for place in range(out_ref.shape[0]):
            out_ref[place] = total


def inverse_kernel(weight_ref, blocks_ref, *refs):
    parts = sum(ref.ndim == 2 for ref in refs[:-1])
    field_refs, copied_refs, full_ref = refs[:parts], refs[parts:-1], refs[-1]
    assemble(blocks_ref, full_ref, 0)
    real, imag = complex_parts(multiply(full_ref[...], weight_ref[...]))
    real, imag = real.astype(jnp.bfloat16), imag.astype(jnp.bfloat16)
    cols = real.shape[0]
    half = cols // parts
    for part, field_ref in enumerate(field_refs):
        field_ref[:half] = real[part * half : (part + 1) * half]
        field_ref[half:] = imag[part * half : (part + 1) * half]
    for copied_ref in copied_refs:
        for place in range(copied_ref.shape[0]):
            copied_ref[place, :cols] = real
            copied_ref[place, cols:] = imag


def nothing(shapes):
    return list(
        pl.pallas_call(
            lambda *refs: None, out_shape=shapes, out_specs=[ANY] * len(shapes), name="nothing"
        )()
    )


def held(array):
    return pltpu.with_memory_space_constraint(array, pltpu.VMEM)


def far(array):
    return pltpu.with_memory_space_constraint(array, pltpu.HBM)


def local(right_side, inverse, coupling, image_offset, image_count, phase_exponent):
    layers, rows, _, cols = right_side.shape
    slots, unknowns = coupling.shape[1], coupling.shape[4]
    peers = lax.axis_size("angle")
    chips = lax.axis_size("layer") // CORES
    chip, core = jnp.divmod(lax.axis_index("layer"), CORES)
    deep = CORES * layers
    width = cols // CORES
    wide = 2 * width

    def ordered(mine, given):
        return jnp.where(core == 0, jnp.concatenate([mine, given]), jnp.concatenate([given, mine]))

    right = right_side.reshape(layers, rows, 2, CORES, width).transpose(3, 0, 2, 4, 1)
    split = right.reshape(CORES, layers, wide, rows)
    right = ordered(
        jnp.where(core == 0, split[0], split[1]), swap(jnp.where(core == 0, split[1], split[0]))
    )
    kinds = jnp.where(lax.iota(jnp.int32, slots) < image_count[:, None], image_offset, 0)
    both = jnp.stack([kinds, phase_exponent], 1)
    both = ordered(both, swap(both))
    begin = right_side[0].transpose(1, 2, 0).reshape(CORES * wide, rows)
    tied = lax.optimization_barrier((right, both, begin, inverse, coupling))
    right, both, begin, late_inverse, late_coupling = tied
    other_coupling, other_inverse = swap(late_coupling), swap(late_inverse)
    plan = jnp.concatenate([both[:, 0], jnp.full((1, slots), core, jnp.int32)]).astype(jnp.float32)
    plan = jnp.broadcast_to(plan[..., None, None], (deep + 1, slots, 8, 128))
    angle = ((core * width + lax.iota(jnp.int32, width)) // NRHS).astype(jnp.float32)
    phase = (2.0 * math.pi / ANGLES) * both[:, 1].astype(jnp.float32)[:, :, None] * (angle + 0.5)
    table = jnp.stack([jnp.cos(phase), jnp.sin(phase)], 2)
    table = jnp.broadcast_to(table[..., None], table.shape + (128,))

    params = pltpu.CompilerParams(vmem_limit_bytes=LIMIT)
    field_shape = jax.ShapeDtypeStruct((wide, rows), jnp.bfloat16)
    copied_shape = jax.ShapeDtypeStruct((peers, wide, rows), jnp.bfloat16)
    full_scratch = pltpu.VMEM((wide, unknowns), jnp.bfloat16)

    def cost(planes):
        return pl.CostEstimate(
            flops=4 * wide * rows * unknowns * planes,
            bytes_accessed=4 * rows * unknowns * planes,
            transcendentals=0,
        )

    def images(layer, kind, base, blocks, ahead=None):
        blocks = blocks if ahead is None else [*blocks, ahead]
        first_weights = pltpu.VMEM(coupling.shape[2:], coupling.dtype)
        part = jax.ShapeDtypeStruct((wide, rows), jnp.float32)
        return pl.pallas_call(
            functools.partial(image_kernel, layer, kind, base.ndim == 3, kind == 2 or ahead is not None),
            out_shape=copied_shape if kind == 1 else [part, first_weights],
            in_specs=[VMEM] * 2 + [ANY] * 2 + [VMEM] * (1 + len(blocks)),
            out_specs=VMEM if kind == 1 else [VMEM] * 2,
            scratch_shapes=[
                pltpu.VMEM((wide, rows), jnp.float32),
                full_scratch,
                pltpu.VMEM((slots, 2, rows, unknowns), jnp.bfloat16),
                pltpu.SemaphoreType.DMA((slots + 1,)),
            ],
            compiler_params=params,
            cost_estimate=cost(slots // 2),
            name="images_%d" % kind,
        )(plan, table, far(coupling), far(other_coupling), base, *blocks)

    def invert(blocks, weights, last):
        parts = blocks.shape[1] // wide
        out_shape = [field_shape] * parts + [jax.ShapeDtypeStruct(blocks.shape, jnp.bfloat16)] * (not last)
        return pl.pallas_call(
            inverse_kernel,
            out_shape=out_shape,
            in_specs=[VMEM] * 2,
            out_specs=[VMEM] * len(out_shape),
            scratch_shapes=[pltpu.VMEM((parts * wide, unknowns), jnp.bfloat16)],
            compiler_params=params,
            cost_estimate=cost(1),
            name="invert",
        )(held(weights), blocks)

    def load(layer, other, after):
        return pl.pallas_call(
            functools.partial(load_kernel, layer),
            out_shape=pltpu.VMEM(inverse.shape[1:], inverse.dtype),
            in_specs=[VMEM] + [ANY] * 3,
            out_specs=VMEM,
            scratch_shapes=[pltpu.SemaphoreType.DMA],
            compiler_params=pltpu.CompilerParams(vmem_limit_bytes=2**20),
            cost_estimate=pl.CostEstimate(flops=0, bytes_accessed=inverse.size * 2, transcendentals=0),
            name="load",
        )(plan, far(inverse), far(other), after)

    def run(start, latest, earlier):
        fields = []
        for layer in range(start, deep):
            base, ahead = (right, None) if earlier is None else images(layer, 2, right, earlier)
            copied = images(layer, 1, base, latest, None if ahead is None else held(ahead))
            if layer + 1 < deep:
                field, next_copied = invert(gather(copied), load(layer, other_inverse, copied), False)
                fields.append(field)
                earlier, latest = latest, [gather(next_copied)]
        return [*fields, copied, *latest]

    def finish(copied):
        return list(invert(gather(copied), load(deep - 1, other_inverse, copied), True))

    def only(here, shapes, function, *operands):
        return lax.cond(here, function, lambda *_: nothing(shapes), *operands)

    found = []
    field = earlier = None
    for number in range(chips):
        if number == 0:
            gathered = jax.ShapeDtypeStruct((peers, CORES * wide, rows), jnp.bfloat16)

            def layer_zero(begin):
                copied = copies(begin, peers)
                *fields, copied = invert(gather(copied), load(0, inverse, copied), False)
                return [*fields, gather(copied)]

            begin, _ = lax.optimization_barrier((begin, table))
            shapes = [field_shape] * CORES + [gathered]
            *zero, latest = only((chip == 0) & (core == 0), shapes, layer_zero, begin)
            pairs = [(b, peers + b) for b in range(peers)]
            given = lax.ppermute(latest, ("layer", "angle"), pairs)
            start, function, operands = 1, lambda *latest: run(1, latest, None), (latest, given)
        else:

            def function(field, earlier):
                return run(0, [gather(copies(field, peers))], [earlier])

            start, operands = 0, (field, earlier)
        here = chip == number
        shapes = [field_shape] * (deep - start - 1) + [copied_shape] * 2
        *fields, copied, latest = only(here, shapes, function, *operands)
        if number + 1 < chips:
            earlier = shift(latest, number)
        (last,) = only(here, [field_shape], finish, copied)
        found.append((zero[:1] if start else []) + fields + [last])
        if number + 1 < chips:
            field = shift(last, number)

    chosen = []
    for layer in range(deep):
        value = found[0][layer]
        for number in range(1, chips):
            value = jnp.where(chip == number, found[number][layer], value)
        chosen.append(value)
    low, high = jnp.stack(chosen[:layers]), jnp.stack(chosen[layers:])
    mine = jnp.where(core == 0, low, high)
    given = swap(jnp.where(core == 0, high, low))
    first_given = jnp.where(chip == 0, jnp.where(core == 0, zero[1], given[0]), given[0])
    given = jnp.concatenate([first_given[None], given[1:]])
    result = jnp.where(core == 0, jnp.stack([mine, given]), jnp.stack([given, mine]))
    result = result.reshape(CORES, layers, 2, width, rows).transpose(1, 4, 2, 0, 3)
    return result.reshape(layers, rows, 2, cols)


def solution(mesh):
    placed = (
        P("layer", "angle", None, None),
        P("layer", None, "angle", None),
        P("layer", None, None, "angle", None),
        P("layer", None),
        P("layer"),
        P("layer", None),
    )
    return jax.shard_map(
        local,
        mesh=mesh,
        in_specs=placed,
        out_specs=P("layer", "angle", None, None),
        check_vma=False,
    )
```
